256 devices in a mesh: mp: 4 (over z_hi, core), fsdp: 64 (over x, y, z_lo).
Axes of the slice: x: 4, y: 4, z: 8 (z_hi: 2, z_lo: 4; z = z_hi * 4 + z_lo), core: 2. Of those that a mesh axis runs over, the one named last changes fastest.
Arguments:
- hidden_in: bfloat16 [4, 49152, 5120], P('mp', 'fsdp'), may hold values from -16 to 16
- gain_in: bfloat16 [4, 5120], P('mp'), may hold values from 0.099609375 to 1.8984375
- w_key: bfloat16 [4, 5120, 512], P('mp', 'fsdp'), may hold values from -0.078125 to 0.078125
- key_gain: bfloat16 [4, 128], P('mp'), may hold values from 0.099609375 to 1.8984375
- partner: int32 [4], replicated, may hold values from 0 to 3, as said below
Outputs:
- grad_key: float32 [4, 5120, 512], P('mp', 'fsdp')
- grad_key_gain: float32 [4, 128], P('mp')
- distill_loss: float32 [4], P('mp')
The draws below stay inside these ranges and needn't reach their ends.
Inputs may be any that keep to these rules, and one draw needn't show every extreme that they name: partner[m] differs from m.
All inputs are finite; a program needn't handle non-finite values.
Results may differ from the reference program's by a relative error of at most 0.0016.
Values may be sent and summed in bfloat16 or wider, within the bound.
A program may use at most 128 MiB of HBM per device.

```python
import jax
import jax.numpy as jnp
from jax import lax

D = 5120
HD = 128
KW = 512
MODELS = 4
TOKENS = 49152


def draw_partner(key, part):
    key = jax.random.fold_in(key, 5)
    offsets = jax.random.randint(key, (MODELS,), 1, MODELS)
    return ((jnp.arange(MODELS) + offsets) % MODELS).astype(jnp.int32)


def spiked(drawn, own_key, source, target, blocks, factor):
    owner, partner = [(jnp.arange(drawn.shape[position]) // (drawn.shape[position] // blocks)).reshape([-1 if axis == position else 1 for axis in range(drawn.ndim)]) for position in (source, target)]
    chosen = jax.random.permutation(own_key, blocks)[partner]
    strong = (owner == chosen) | (owner == (partner + blocks // 2) % blocks)
    return jnp.where(strong, factor * drawn, drawn)


def shard_levels(stream_key, dims, cuts, smallest, high):
    loudness, own = 1.0, jax.random.fold_in(stream_key, 6)
    for axis_at, parts in cuts:
        draws = jnp.exp(jax.random.uniform(jax.random.fold_in(own, axis_at), (parts,), jnp.float32, smallest / len(cuts), high / len(cuts)))
        loudness = loudness * jnp.repeat(draws, dims[axis_at] // parts).reshape([-1 if axis == axis_at else 1 for axis in range(len(dims))])
    return loudness


def gaussian(own_key, extent, scale, reach, split=(), held_as=jnp.bfloat16):
    level = shard_levels(own_key, extent, split, -0.22, 0.18) if split else 1.0
    result = jax.random.normal(own_key, extent, jnp.float32) * scale * level
    return jnp.minimum(jnp.maximum(result, -reach), reach).astype(held_as)


def gaussian_with(own_key, shape, deviation, bound, cuts, heavy, dtype=jnp.bfloat16):
    array = deviation * jax.random.normal(own_key, shape, jnp.float32)
    if cuts:
        array = array * shard_levels(own_key, shape, cuts, -0.22, 0.18)
    return jnp.clip(spiked(array, jax.random.fold_in(own_key, 3), *heavy), -bound, bound).astype(dtype)


def setup_inputs(seed: int = 0) -> dict:
    arg_keys = jax.random.split(jax.random.key(seed), 6)
    return {
        "hidden_in": gaussian_with(arg_keys[0], (MODELS, TOKENS, D), 1.0, 16.0, ((0, 4), (1, 64)), (1, 2, 64, 4.0)),
        "gain_in": jnp.clip(1.0 + 0.18 * jax.random.normal(arg_keys[1], (MODELS, D), jnp.float32), 0.099609375, 1.8984375).astype(jnp.bfloat16),
        "w_key": gaussian(arg_keys[2], (MODELS, D, KW), D ** -0.5, 0.078125, ((0, 4), (1, 64))),
        "key_gain": jnp.clip(1.0 + 0.18 * jax.random.normal(arg_keys[3], (MODELS, HD), jnp.float32), 0.099609375, 1.8984375).astype(jnp.bfloat16),
        "partner": draw_partner(jax.random.fold_in(arg_keys[5], 71), 0),
    }


def norm_input(hidden, gain):
    values = hidden.astype(jnp.float32)
    scale = lax.rsqrt(lax.optimization_barrier(jnp.mean(values * values, axis=-1, keepdims=True)) + 1e-06)
    return (values * scale * gain.astype(jnp.float32)).astype(jnp.bfloat16)

def norm_keys(keys, gain):
    heads = keys.reshape(keys.shape[0], -1, gain.shape[0])
    inverse = lax.rsqrt(lax.optimization_barrier(jnp.mean(heads * heads, axis=-1, keepdims=True)) + 1e-06)
    return (heads, inverse, heads * inverse * gain.astype(jnp.float32))

def distill_terms(keys_student, keys_teacher, gain_student, gain_teacher):
    heads, inverse, out_student = norm_keys(keys_student, gain_student)
    unused_heads, unused_inverse, out_teacher = norm_keys(keys_teacher, gain_teacher)
    differ = out_student - out_teacher
    loss_sum = jnp.sum(differ * differ)
    upstream = differ / keys_student.shape[1]
    weighted = upstream * gain_student.astype(jnp.float32)
    inner = lax.optimization_barrier(jnp.sum(weighted * heads, axis=-1, keepdims=True))
    grad_heads = weighted * inverse - heads * inverse * inverse * inverse * inner / heads.shape[-1]
    grad_gain = lax.optimization_barrier(jnp.sum(upstream * heads * inverse, axis=(0, 1)))
    return (loss_sum, grad_heads.reshape(keys_student.shape).astype(jnp.bfloat16), grad_gain)

def reference(hidden_in, gain_in, w_key, key_gain, partner):
    grads = []
    gains = []
    losses = []
    for model in range(MODELS):
        teacher = partner[model]
        normed_student = norm_input(hidden_in[model], gain_in[model])
        normed_teacher = norm_input(hidden_in[model], gain_in[teacher])
        keys_student = jnp.dot(normed_student, w_key[model], preferred_element_type=jnp.float32)
        keys_teacher = jnp.dot(normed_teacher, w_key[teacher], preferred_element_type=jnp.float32)
        loss_sum, grad_keys, grad_gain = distill_terms(keys_student, keys_teacher, key_gain[model], key_gain[teacher])
        grads.append(jnp.dot(normed_student.T, grad_keys, preferred_element_type=jnp.float32))
        gains.append(grad_gain)
        losses.append(loss_sum / (TOKENS * KW))
    return (jnp.stack(grads), jnp.stack(gains), jnp.stack(losses))
```

```python
import jax
import jax.numpy as jnp
from jax import lax
from jax.experimental import pallas as pl
from jax.experimental.pallas import tpu as pltpu
from jax.sharding import PartitionSpec as P

MESH = pl.DeviceIdType.MESH
F32, BF16, I16 = jnp.float32, jnp.bfloat16, jnp.int16
D, KW, HD, TOK, CHUNK = 5120, 512, 128, 768, 80
HALF = KW // 2
SLAB = D // 4
EPS = 1e-6
TOP = 32767.0
ROWS = (pl.ds(0, 32), pl.ds(32, 32), pl.ds(64, 16))
NSEM = 420


def kernel(
    hid, gains, w, partner, grad, stats,
    wall0, wall1, ns, nt, nst, ks, kt, gk, gt, q, sc, g4, stat4,
    r1x, r1y, r1z, s1, acc, q2x, q2y, q2z, r2x, r2y, r2z, s2o, s2,
    q3x, q3y, q3z, r3x, r3y, r3z, s3o, s3, ssem, rsem, lsem,
):
    m, f = lax.axis_index("mp"), lax.axis_index("fsdp")
    x, y = f // 16, (f // 4) % 4
    zl, zh, c = f % 4, m // 2, m % 2
    z = zh * 4 + zl

    def dev(px, py, pz, pc):
        pz = (pz + 8) % 8
        return ((pz // 4) * 2 + pc, (((px + 4) % 4) * 4 + (py + 4) % 4) * 4 + pz % 4)

    def at_x(d):
        return dev(x + d, y, z, c)

    def at_y(d):
        return dev(x, y + d, z, c)

    def at_z(d):
        return dev(x, y, z + d, c)

    def at_line(d):
        return dev(x, y, zh * 4 + (zl + d) % 4, c)

    walls = (wall0, wall1)
    sibling = dev(x, y, z, 1 - c)
    others = (sibling, dev(x, y, z + 4, c), dev(x, y, z + 4, 1 - c))
    slot_of = (zh * 2 + 1 - c, (1 - zh) * 2 + c, (1 - zh) * 2 + 1 - c)

    used = [0]
    pending = []

    def take(n=1):
        used[0] += n
        assert used[0] <= NSEM
        return used[0] - n

    def copy(src, dst, to, si, ri):
        return pltpu.make_async_remote_copy(
            src_ref=src, dst_ref=dst, send_sem=ssem.at[si], recv_sem=rsem.at[ri],
            device_id=to, device_id_type=MESH,
        )

    def send(src, dst, to, ri=None):
        si = take()
        ri = si if ri is None else ri
        one = copy(src, dst, to, si, ri)
        one.start()
        pending.append(one)
        return ri

    def arrived(ref, ri):
        copy(ref, ref, sibling, ri, ri).wait_recv()

    loads = [
        pltpu.make_async_copy(w.at[0, :, pl.ds(HALF * ph, HALF)], walls[ph].at[m, x, y, zl], lsem.at[ph])
        for ph in range(2)
    ]
    for one in loads:
        one.start()
    hidden_loads = [
        pltpu.make_async_copy(hid.at[0, :, pl.ds(SLAB * s, SLAB)], nt.at[s], lsem.at[2 + s]) for s in range(4)
    ]
    for one in hidden_loads:
        one.start()
    barrier = pltpu.get_barrier_semaphore()
    peers = [at_x(d) for d in (1, 2, 3)] + [at_y(d) for d in (1, 2, 3)] + [at_z(1), at_z(-1)]
    peers += [at_line(d) for d in (1, 2, 3)] + list(others)
    for one in peers:
        pl.semaphore_signal(barrier, inc=1, device_id=one, device_id_type=MESH)
    g4[m] = gains[...]
    pl.semaphore_wait(barrier, len(peers))

    def model(zz):
        return (zz // 4) * 2 + c

    def gather(ph):
        back = take(2)

        def chunk(px, py, part):
            return walls[ph].at[m, px, py, zl, ROWS[part]]

        def block(part, zz, lane=None, half=None):
            some = slice(None) if half is None else pl.ds(2 * half, 2)
            mod, low, rows = model(zz), zz % 4, ROWS[part]
            if lane is None:
                return walls[ph].at[mod, some, :, low, rows]
            lane = (lane + 4) % 4
            if part == 0:
                return walls[ph].at[mod, lane, some, low, rows]
            return walls[ph].at[mod, some, lane, low, rows]

        at = (at_x, at_y)
        pos = (x, y)

        first = []
        for part, hop in ((0, at_y), (1, at_x), (2, at_x)):
            mine = chunk(x, y, part)
            first.append([send(mine, mine, hop(d)) for d in (1, 2, 3)])
        yield

        ring = {}
        last = {}

        def z_own(part, lane):
            mine = block(part, z, lane)
            up = send(mine, mine, at_z(1))
            down = send(mine, mine, at_z(-1))
            ring[part] = (up, down)

        def z_step(part, lane, j):
            up, down = ring[part]
            if j < 4:
                for sign, ri in ((-1, up), (1, down)):
                    got = block(part, (z + sign * j + 8) % 8, lane)
                    arrived(got, ri)
                half = {1: None, 2: None, 3: 0}[j]
                one = block(part, (z - j + 8) % 8, lane, half)
                up = send(one, one, at_z(1))
                half = {1: None, 2: None, 3: 1}[j]
                one = block(part, (z + j) % 8, lane, half)
                down = send(one, one, at_z(-1))
                ring[part] = (up, down)
            else:
                arrived(block(part, (z + 4) % 8, lane, 0), up)
                arrived(block(part, (z + 4) % 8, lane, 1), down)

        def l_own(part, j):
            one = block(part, (z + j + 8) % 8, pos[part])
            last[part, j] = (send(one, one, at[part](1)), send(one, one, at[part](-1)))

        def l_pass(part, j):
            zz = (z + j + 8) % 8
            up, down = last[part, j]
            arrived(block(part, zz, pos[part] - 1), up)
            one = block(part, zz, pos[part] - 1, 0)
            up = send(one, one, at[part](1))
            arrived(block(part, zz, pos[part] + 1), down)
            one = block(part, zz, pos[part] + 1, 1)
            down = send(one, one, at[part](-1))
            last[part, j] = (up, down)

        def hand_over(part, j):
            zz = (z + j + 8) % 8
            one = block(part, zz)
            send(one, one, sibling, back + zz // 4)

        def l_end(part, j):
            zz = (z + j + 8) % 8
            up, down = last[part, j]
            arrived(block(part, zz, pos[part] + 2, 0), up)
            arrived(block(part, zz, pos[part] + 2, 1), down)
            hand_over(part, j)

        for d in (1, 2, 3):
            arrived(chunk(x, (y - d + 4) % 4, 0), first[0][d - 1])
        z_own(0, x)
        l_own(0, 0)
        for d in (1, 2, 3):
            arrived(chunk((x - d + 4) % 4, y, 1), first[1][d - 1])
        z_own(1, y)
        l_own(1, 0)
        for d in (1, 2, 3):
            arrived(chunk((x - d + 4) % 4, y, 2), first[2][d - 1])
        mine = walls[ph].at[m, :, y, zl, ROWS[2]]
        second = [send(mine, mine, at_y(d)) for d in (1, 2, 3)]
        yield
        for j in range(1, 5):
            for part in (0, 1):
                z_step(part, pos[part], j)
                for sign in (-1, 1) if j < 4 else (1,):
                    l_own(part, sign * j)
                yield
            if j == 1:
                for d in (1, 2, 3):
                    arrived(walls[ph].at[m, :, (y - d + 4) % 4, zl, ROWS[2]], second[d - 1])
                z_own(2, None)
                hand_over(2, 0)
            else:
                z_step(2, None, j - 1)
                hand_over(2, j - 1)
                hand_over(2, 1 - j)
            yield
            for part in (0, 1):
                for sign in (-1, 1) if j > 1 else (1,):
                    l_pass(part, sign * (j - 1))
                if j > 1:
                    for sign in (-1, 1) if j > 2 else (1,):
                        l_end(part, sign * (j - 2))
                yield
        for part in (0, 1):
            l_pass(part, 4)
            for sign in (-1, 1):
                l_end(part, sign * 3)
            yield
        z_step(2, None, 4)
        hand_over(2, 4)
        for part in (0, 1):
            l_end(part, 4)
        yield
        for h in range(2):
            arrived(walls[ph].at[h * 2 + 1 - c], back + h)

    def teacher():
        return partner[m]

    got_gain = []

    def share_gains():
        for to in others:
            got_gain.append(send(g4.at[m], g4.at[m], to))

    def wait_inputs():
        for slot, ri in zip(slot_of, got_gain):
            arrived(g4.at[slot], ri)
        for one in hidden_loads:
            one.wait()

    def prep(t):
        def rows16(i, carry):
            rows = pl.ds(pl.multiple_of(t * 128 + i * 16, 16), 16)
            total = jnp.zeros((16, 1), F32)
            for s in range(4):
                v = nt[s, rows, :].astype(F32)
                total = total + jnp.sum(v * v, axis=-1, keepdims=True)
            scale = lax.rsqrt(total / D + EPS)
            p = teacher()
            for s in range(4):
                v = nt[s, rows, :].astype(F32) * scale
                ns[s, rows, :] = (v * g4[m, s]).astype(BF16)
                nt[s, rows, :] = (v * g4[p, s]).astype(BF16)
            return carry

        lax.fori_loop(0, 8, rows16, 0)

        def turn(s, carry):
            nst[s, :, pl.ds(t * 128, 128)] = ns[s, pl.ds(t * 128, 128), :].T
            return carry

        lax.fori_loop(0, 4, turn, 0)

    def keys(ph, which, s):
        left, out = ((ns, ks), (nt, kt))[which]
        who = m if which == 0 else teacher()
        right = walls[ph][who, s].reshape(SLAB, HALF)
        part = jnp.dot(left[s], right, preferred_element_type=F32)
        if s == 0:
            out[...] = part
        else:
            out[...] += part

    def distill(ph):
        p = teacher()

        def tile(i, carry):
            loss, ggain = carry
            rows = pl.ds(pl.multiple_of(i * 64, 64), 64)
            own_gain, far_gain = g4[m, 4][:, :HD], g4[p, 4][:, :HD]
            for h in range(2):
                cols = pl.ds(h * HD, HD)
                a, b = ks[rows, cols], kt[rows, cols]
                inv_a = lax.rsqrt(jnp.sum(a * a, axis=-1, keepdims=True) / HD + EPS)
                inv_b = lax.rsqrt(jnp.sum(b * b, axis=-1, keepdims=True) / HD + EPS)
                differ = a * inv_a * own_gain - b * inv_b * far_gain
                loss = loss + jnp.sum(differ * differ, axis=0, keepdims=True)
                up = differ / KW
                weighted = up * own_gain
                inner = jnp.sum(weighted * a, axis=-1, keepdims=True)
                g = weighted * inv_a - a * (inv_a * inv_a * inv_a * inner / HD)
                gk[rows, cols] = g.astype(BF16)
                ggain = ggain + jnp.sum(up * a * inv_a, axis=0, keepdims=True)
            return loss, ggain

        zero = jnp.zeros((1, HD), F32)
        loss, ggain = lax.fori_loop(0, TOK // 64, tile, (zero, zero))
        if ph == 0:
            stat4[0, 0:1] = loss
            stat4[0, 1:2] = ggain
        else:
            stat4[0, 0:1] += loss
            stat4[0, 1:2] += ggain

    base1 = [take(9) for _ in range(2)]
    base1s = [take(9) for _ in range(2)]

    def quantize(read, write, n):
        def most(i, top):
            v = jnp.abs(read(i))
            return jnp.maximum(top, jnp.max(v.reshape(-1, HALF), axis=0, keepdims=True))

        top = lax.fori_loop(0, n, most, jnp.full((1, HALF), 1e-30, F32))
        factor = TOP / top

        def store(i, carry):
            write(i, jnp.round(read(i) * factor).astype(jnp.int32).astype(I16))
            return carry

        lax.fori_loop(0, n, store, 0)
        return top / TOP

    def grads(ph, d):
        s = (x + d) % 4
        gt[...] = jnp.dot(nst[s], gk[...], preferred_element_type=F32).reshape(4, 4, CHUNK, HALF)

        def read(i):
            return gt[i // 4, i % 4]

        def write(i, v):
            q[ph, s, i // 4, i % 4] = v

        sc[ph, s] = quantize(read, write, 16)
        if d < 4:
            one = copy(q.at[ph, s, :, :, ROWS[0]], r1x.at[ph, d - 1], at_x(d), base1[ph] + d - 1, base1[ph] + d - 1)
            one.start()
            pending.append(one)

    def grads_send(ph):
        for d in (1, 2, 3):
            k = base1[ph] + 2 + d
            one = copy(q.at[ph, :, (y + d) % 4, :, ROWS[1]], r1y.at[ph, d - 1], at_y(d), k, k)
            one.start()
            pending.append(one)
            k = base1[ph] + 5 + d
            one = copy(q.at[ph, :, :, (zl + d) % 4, ROWS[2]], r1z.at[ph, d - 1], at_line(d), k, k)
            one.start()
            pending.append(one)
        for a, hop in enumerate((at_x, at_y, at_line)):
            for d in (1, 2, 3):
                k = base1s[ph] + 3 * a + d - 1
                one = copy(sc.at[ph], s1.at[ph, a, d - 1], hop(d), k, k)
                one.start()
                pending.append(one)

    def wait1(ph, a, ref):
        for d in range(3):
            arrived(ref.at[ph, d], base1[ph] + 3 * a + d)
            arrived(s1.at[ph, a, d], base1s[ph] + 3 * a + d)

    def i2f(v):
        return v.astype(jnp.int32).astype(F32)

    def stage2(ph):
        ids = {}
        wait1(ph, 0, r1x)

        def add0(i, carry):
            a, b = i // 4, i % 4
            v = i2f(q[ph, x, a, b, ROWS[0]]) * sc[ph, x]
            for d in range(3):
                v = v + i2f(r1x[ph, d, a, b]) * s1[ph, 0, d, x]
            acc[a, b] = v
            return carry

        lax.fori_loop(0, 16, add0, 0)

        def write0(i, v):
            q2x[ph, i // 4, i % 4] = v

        s2o[ph, 0] = quantize(lambda i: acc[i // 4, i % 4], write0, 16)
        for d in (1, 2, 3):
            ids[0, d] = (
                send(q2x.at[ph, (y + d) % 4], r2x.at[ph, d - 1], at_y(d)),
                send(s2o.at[ph, 0], s2.at[ph, 0, d - 1], at_y(d)),
            )
        wait1(ph, 1, r1y)

        def add1(i, carry):
            a, b = i // 4, i % 4
            v = i2f(q[ph, a, y, b, ROWS[1]]) * sc[ph, a]
            for d in range(3):
                v = v + i2f(r1y[ph, d, a, b]) * s1[ph, 1, d, a]
            acc[a, b] = v
            return carry

        lax.fori_loop(0, 16, add1, 0)

        def write1(i, v):
            q2y[ph, i // 4, i % 4] = v

        s2o[ph, 1] = quantize(lambda i: acc[i // 4, i % 4], write1, 16)
        for d in (1, 2, 3):
            ids[1, d] = (
                send(q2y.at[ph, (x + d) % 4], r2y.at[ph, d - 1], at_x(d)),
                send(s2o.at[ph, 1], s2.at[ph, 1, d - 1], at_x(d)),
            )
        wait1(ph, 2, r1z)

        def add2(i, carry):
            a, b = i // 4, i % 4
            v = i2f(q[ph, a, b, zl, ROWS[2]]) * sc[ph, a]
            for d in range(3):
                v = v + i2f(r1z[ph, d, a, b]) * s1[ph, 2, d, a]
            acc[a, b, 0:16] = v
            return carry

        lax.fori_loop(0, 16, add2, 0)

        def write2(i, v):
            q2z[ph, i // 4, i % 4] = v

        s2o[ph, 2] = quantize(lambda i: acc[i // 4, i % 4, 0:16], write2, 16)
        for d in (1, 2, 3):
            ids[2, d] = (
                send(q2z.at[ph, (x + d) % 4], r2z.at[ph, d - 1], at_x(d)),
                send(s2o.at[ph, 2], s2.at[ph, 2, d - 1], at_x(d)),
            )
        return ids

    def stage3(ph, ids):
        out = {}
        for a, (own, got, mid, pos, hop, n) in enumerate((
            (q2x.at[ph, y], r2x, q3x, zl, at_line, 32),
            (q2y.at[ph, x], r2y, q3y, zl, at_line, 32),
            (q2z.at[ph, x], r2z, q3z, y, at_y, 16),
        )):
            for d in (1, 2, 3):
                arrived(got.at[ph, d - 1], ids[a, d][0])
                arrived(s2.at[ph, a, d - 1], ids[a, d][1])
            for b in range(4):
                v = i2f(own[b]) * s2o[ph, a]
                for d in range(3):
                    v = v + i2f(got[ph, d, b]) * s2[ph, a, d]
                acc[0, b, 0:n] = v

            def write(i, v, mid=mid):
                mid[ph, i] = v

            s3o[ph, a] = quantize(lambda i, n=n: acc[0, i, 0:n], write, 4)
            into = (r3x, r3y, r3z)[a]
            for d in (1, 2, 3):
                out[a, d] = (
                    send(mid.at[ph, (pos + d) % 4], into.at[ph, d - 1], hop(d)),
                    send(s3o.at[ph, a], s3.at[ph, a, d - 1], hop(d)),
                )
        return out

    def finish(ph, ids):
        for a, (own, got, n, row) in enumerate((
            (q3x.at[ph, zl], r3x, 32, 0), (q3y.at[ph, zl], r3y, 32, 32), (q3z.at[ph, y], r3z, 16, 64),
        )):
            v = i2f(own[...]) * s3o[ph, a]
            for d in (1, 2, 3):
                arrived(got.at[ph, d - 1], ids[a, d][0])
                arrived(s3.at[ph, a, d - 1], ids[a, d][1])
                v = v + i2f(got[ph, d - 1]) * s3[ph, a, d - 1]
            grad[row : row + n, HALF * ph : HALF * ph + HALF] = v

    def stat_send(a, hop):
        return [send(stat4.at[4 * a], stat4.at[4 * a + d], hop(d)) for d in (1, 2, 3)]

    def stat_add(a, ids):
        v = stat4[4 * a]
        for d in (1, 2, 3):
            arrived(stat4.at[4 * a + d], ids[d - 1])
            v = v + stat4[4 * a + d]
        return v

    def together(events, pieces):
        pieces = list(pieces)
        for _ in events:
            if pieces:
                pieces.pop(0)()
        for one in pieces:
            one()

    for one in loads:
        one.wait()
    one_a, one_b = gather(0), gather(1)
    next(one_a)
    share_gains()
    next(one_a)
    next(one_b)
    stat4[0] = jnp.zeros((8, HD), F32)
    together(one_a, [wait_inputs] + [lambda t=t: prep(t) for t in range(6)] + [lambda: next(one_b)])

    def work(ph):
        for which in (0, 1):
            for s in range(4):
                yield lambda which=which, s=s: keys(ph, which, s)
        yield lambda: distill(ph)
        for d in (1, 2, 3, 4):
            yield lambda d=d: grads(ph, d)
        yield lambda: grads_send(ph)

    together(one_b, work(0))
    for one in work(1):
        one()
    sid = stat_send(0, at_x)
    ids_a = stage2(0)
    stat4[4] = stat_add(0, sid)
    sid = stat_send(1, at_y)
    ids_a = stage3(0, ids_a)
    ids_b = stage2(1)
    stat4[8] = stat_add(1, sid)
    sid = stat_send(2, at_line)
    finish(0, ids_a)
    ids_b = stage3(1, ids_b)
    total = stat_add(2, sid)
    loss = jnp.sum(total[0:1], axis=-1, keepdims=True) / float(TOK * 64 * KW)
    stats[...] = jnp.concatenate([jnp.broadcast_to(loss, (1, HD)), total[1:8]], axis=0)
    finish(1, ids_b)
    for one in pending:
        one.wait_send()


def local(hidden_in, gain_in, w_key, key_gain, partner):
    gains = jnp.concatenate(
        [gain_in.astype(F32).reshape(4, 1, SLAB), jnp.pad(key_gain.astype(F32), ((0, 0), (0, SLAB - HD))).reshape(1, 1, SLAB)]
    )
    vmem, dma = pltpu.VMEM, pltpu.SemaphoreType.DMA
    grad, stats = pl.pallas_call(
        kernel,
        out_shape=(jax.ShapeDtypeStruct((CHUNK, KW), F32), jax.ShapeDtypeStruct((8, HD), F32)),
        in_specs=[
            pl.BlockSpec(memory_space=pl.ANY),
            pl.BlockSpec(memory_space=pltpu.VMEM),
            pl.BlockSpec(memory_space=pl.ANY),
            pl.BlockSpec(memory_space=pltpu.SMEM),
        ],
        out_specs=(pl.BlockSpec(memory_space=pltpu.VMEM), pl.BlockSpec(memory_space=pltpu.VMEM)),
        scratch_shapes=[
            vmem((4, 4, 4, 4, CHUNK, HALF), BF16),
            vmem((4, 4, 4, 4, CHUNK, HALF), BF16),
            vmem((4, TOK, SLAB), BF16),
            vmem((4, TOK, SLAB), BF16),
            vmem((4, SLAB, TOK), BF16),
            vmem((TOK, HALF), F32),
            vmem((TOK, HALF), F32),
            vmem((TOK, HALF), BF16),
            vmem((4, 4, CHUNK, HALF), F32),
            vmem((2, 4, 4, 4, CHUNK, HALF), I16),
            vmem((2, 4, 1, HALF), F32),
            vmem((4, 5, 1, SLAB), F32),
            vmem((12, 8, HD), F32),
            vmem((2, 3, 4, 4, 32, HALF), I16),
            vmem((2, 3, 4, 4, 32, HALF), I16),
            vmem((2, 3, 4, 4, 16, HALF), I16),
            vmem((2, 3, 3, 4, 1, HALF), F32),
            vmem((4, 4, 32, HALF), F32),
            vmem((2, 4, 4, 32, HALF), I16),
            vmem((2, 4, 4, 32, HALF), I16),
            vmem((2, 4, 4, 16, HALF), I16),
            vmem((2, 3, 4, 32, HALF), I16),
            vmem((2, 3, 4, 32, HALF), I16),
            vmem((2, 3, 4, 16, HALF), I16),
            vmem((2, 3, 1, HALF), F32),
            vmem((2, 3, 3, 1, HALF), F32),
            vmem((2, 4, 32, HALF), I16),
            vmem((2, 4, 32, HALF), I16),
            vmem((2, 4, 16, HALF), I16),
            vmem((2, 3, 32, HALF), I16),
            vmem((2, 3, 32, HALF), I16),
            vmem((2, 3, 16, HALF), I16),
            vmem((2, 3, 1, HALF), F32),
            vmem((2, 3, 3, 1, HALF), F32),
            dma((NSEM,)),
            dma((NSEM,)),
            dma((8,)),
        ],
        compiler_params=pltpu.CompilerParams(
            collective_id=0, has_side_effects=True, vmem_limit_bytes=63 * 2**20
        ),
        cost_estimate=pl.CostEstimate(flops=12 * 10**9, bytes_accessed=10**7, transcendentals=0),
    )(hidden_in, gains, w_key, partner)
    return (grad[None], stats[1:2], stats[0, 0:1])


def solution(mesh):
    return jax.shard_map(
        local,
        mesh=mesh,
        in_specs=(P("mp", "fsdp", None), P("mp", None), P("mp", "fsdp", None), P("mp", None), P()),
        out_specs=(P("mp", "fsdp", None), P("mp", None), P("mp")),
        check_vma=False,
    )
```

```python
import jax
import jax.numpy as jnp
from jax import lax
from jax.experimental import pallas as pl
from jax.experimental.pallas import tpu as pltpu
from jax.sharding import PartitionSpec as P

MESH = pl.DeviceIdType.MESH
F32, BF16, I16 = jnp.float32, jnp.bfloat16, jnp.int16
D, KW, HD, TOK, CHUNK = 5120, 512, 128, 768, 80
HALF = KW // 2
SLAB = D // 4
EPS = 1e-6
TOP = 32767.0
ROWS = (pl.ds(0, 32), pl.ds(32, 32), pl.ds(64, 16))
NSEM = 250
NSEND = 96
LEAD = 10
MAGIC = 12582912.0


def kernel(
    hid, gain, key_gain, w, partner, grad, stats,
    wall0, wall1, ns, nt, nst, ks, kt, gk, q, sc, g4, stat4,
    r1x, r1y, r1z, s1, acc, q2x, q2y, q2z, r2x, r2y, r2z, s2o, s2,
    q3x, q3y, q3z, r3x, r3y, r3z, s3o, s3, ssem, rsem, lsem,
):
    m, f = lax.axis_index("mp"), lax.axis_index("fsdp")
    x, y = f // 16, (f // 4) % 4
    zl, zh, c = f % 4, m // 2, m % 2
    z = zh * 4 + zl

    def dev(px, py, pz, pc):
        pz = (pz + 8) % 8
        return ((pz // 4) * 2 + pc, (((px + 4) % 4) * 4 + (py + 4) % 4) * 4 + pz % 4)

    def at_x(d):
        return dev(x + d, y, z, c)

    def at_y(d):
        return dev(x, y + d, z, c)

    def at_z(d):
        return dev(x, y, z + d, c)

    def at_line(d):
        return dev(x, y, zh * 4 + (zl + d) % 4, c)

    walls = (wall0, wall1)
    sibling = dev(x, y, z, 1 - c)
    others = (sibling, dev(x, y, z + 4, c), dev(x, y, z + 4, 1 - c))
    slot_of = (zh * 2 + 1 - c, (1 - zh) * 2 + c, (1 - zh) * 2 + 1 - c)

    used, sent = [0], [0]
    pending = {}

    def take(n=1):
        used[0] += n
        assert used[0] <= NSEM
        return used[0] - n

    def copy(src, dst, to, si, ri):
        return pltpu.make_async_remote_copy(
            src_ref=src, dst_ref=dst, send_sem=ssem.at[si], recv_sem=rsem.at[ri],
            device_id=to, device_id_type=MESH,
        )

    def send(src, dst, to, ri=None):
        si = sent[0] % NSEND
        sent[0] += 1
        ri = take() if ri is None else ri
        if si in pending:
            pending[si].wait_send()
        one = copy(src, dst, to, si, ri)
        one.start()
        pending[si] = one
        return ri

    def arrived(ref, ri):
        copy(ref, ref, sibling, 0, ri).wait_recv()

    loads = [
        pltpu.make_async_copy(w.at[0, :, pl.ds(HALF * ph, HALF)], walls[ph].at[m, x, y, zl], lsem.at[ph])
        for ph in range(2)
    ]
    for one in loads:
        one.start()
    hidden_loads = [
        pltpu.make_async_copy(hid.at[0, :, pl.ds(SLAB * s, SLAB)], nt.at[s], lsem.at[2 + s]) for s in range(4)
    ]
    for one in hidden_loads:
        one.start()
    barrier = pltpu.get_barrier_semaphore()
    peers = [at_x(d) for d in (1, 2, 3)] + [at_y(d) for d in (1, 2, 3)] + [at_z(1), at_z(-1)]
    peers += [at_line(d) for d in (1, 2, 3)] + list(others)
    for one in peers:
        pl.semaphore_signal(barrier, inc=1, device_id=one, device_id_type=MESH)
    for s in range(4):
        g4[m, s] = gain[:, SLAB * s : SLAB * s + SLAB].astype(F32)
    g4[m, 4] = jnp.zeros((1, SLAB), F32)
    g4[m, 4, :, 0:HD] = key_gain[...].astype(F32)
    pl.semaphore_wait(barrier, len(peers))

    def model(zz):
        return (zz // 4) * 2 + c

    def gather(ph):
        back = take(2)

        def chunk(px, py, part):
            return walls[ph].at[m, px, py, zl, ROWS[part]]

        def block(part, zz, lane=None, half=None):
            some = slice(None) if half is None else pl.ds(2 * half, 2)
            mod, low, rows = model(zz), zz % 4, ROWS[part]
            if lane is None:
                return walls[ph].at[mod, some, :, low, rows]
            lane = (lane + 4) % 4
            if part == 0:
                return walls[ph].at[mod, lane, some, low, rows]
            return walls[ph].at[mod, some, lane, low, rows]

        at = (at_x, at_y)
        pos = (x, y)

        first = []
        for part, hop in ((0, at_y), (1, at_x), (2, at_x)):
            mine = chunk(x, y, part)
            first.append([send(mine, mine, hop(d)) for d in (1, 2, 3)])
        yield

        ring = {}
        last = {}

        def z_own(part, lane):
            mine = block(part, z, lane)
            up = send(mine, mine, at_z(1))
            down = send(mine, mine, at_z(-1))
            ring[part] = (up, down)

        def z_step(part, lane, j):
            up, down = ring[part]
            if j < 4:
                for sign, ri in ((-1, up), (1, down)):
                    got = block(part, (z + sign * j + 8) % 8, lane)
                    arrived(got, ri)
                half = {1: None, 2: None, 3: 0}[j]
                one = block(part, (z - j + 8) % 8, lane, half)
                up = send(one, one, at_z(1))
                half = {1: None, 2: None, 3: 1}[j]
                one = block(part, (z + j) % 8, lane, half)
                down = send(one, one, at_z(-1))
                ring[part] = (up, down)
            else:
                arrived(block(part, (z + 4) % 8, lane, 0), up)
                arrived(block(part, (z + 4) % 8, lane, 1), down)

        def l_own(part, j):
            one = block(part, (z + j + 8) % 8, pos[part])
            last[part, j] = (send(one, one, at[part](1)), send(one, one, at[part](-1)))

        def l_pass(part, j):
            zz = (z + j + 8) % 8
            up, down = last[part, j]
            arrived(block(part, zz, pos[part] - 1), up)
            one = block(part, zz, pos[part] - 1, 0)
            up = send(one, one, at[part](1))
            arrived(block(part, zz, pos[part] + 1), down)
            one = block(part, zz, pos[part] + 1, 1)
            down = send(one, one, at[part](-1))
            last[part, j] = (up, down)

        def hand_over(part, j):
            zz = (z + j + 8) % 8
            one = block(part, zz)
            send(one, one, sibling, back + zz // 4)

        def l_end(part, j):
            zz = (z + j + 8) % 8
            up, down = last[part, j]
            arrived(block(part, zz, pos[part] + 2, 0), up)
            arrived(block(part, zz, pos[part] + 2, 1), down)
            hand_over(part, j)

        for d in (1, 2, 3):
            arrived(chunk(x, (y - d + 4) % 4, 0), first[0][d - 1])
        z_own(0, x)
        l_own(0, 0)
        for d in (1, 2, 3):
            arrived(chunk((x - d + 4) % 4, y, 1), first[1][d - 1])
        z_own(1, y)
        l_own(1, 0)
        for d in (1, 2, 3):
            arrived(chunk((x - d + 4) % 4, y, 2), first[2][d - 1])
        mine = walls[ph].at[m, :, y, zl, ROWS[2]]
        second = [send(mine, mine, at_y(d)) for d in (1, 2, 3)]
        yield
        for j in range(1, 5):
            for part in (0, 1):
                z_step(part, pos[part], j)
                for sign in (-1, 1) if j < 4 else (1,):
                    l_own(part, sign * j)
                yield
            if j == 1:
                for d in (1, 2, 3):
                    arrived(walls[ph].at[m, :, (y - d + 4) % 4, zl, ROWS[2]], second[d - 1])
                z_own(2, None)
                hand_over(2, 0)
            else:
                z_step(2, None, j - 1)
                hand_over(2, j - 1)
                hand_over(2, 1 - j)
            yield
            for part in (0, 1):
                for sign in (-1, 1) if j > 1 else (1,):
                    l_pass(part, sign * (j - 1))
                if j > 1:
                    for sign in (-1, 1) if j > 2 else (1,):
                        l_end(part, sign * (j - 2))
                yield
        for part in (0, 1):
            l_pass(part, 4)
            for sign in (-1, 1):
                l_end(part, sign * 3)
            yield
        z_step(2, None, 4)
        hand_over(2, 4)
        for part in (0, 1):
            l_end(part, 4)
        yield
        for h in range(2):
            arrived(walls[ph].at[h * 2 + 1 - c], back + h)

    def teacher():
        return partner[m]

    got_gain = []

    def share_gains():
        for to in others:
            got_gain.append(send(g4.at[m], g4.at[m], to))

    def wait_inputs():
        for slot, ri in zip(slot_of, got_gain):
            arrived(g4.at[slot], ri)
        for one in hidden_loads:
            one.wait()

    def prep(t):
        def rows16(i, carry):
            rows = pl.ds(pl.multiple_of(t * 128 + i * 16, 16), 16)
            total = jnp.zeros((16, 1), F32)
            for s in range(4):
                v = nt[s, rows, :].astype(F32)
                total = total + jnp.sum(v * v, axis=-1, keepdims=True)
            scale = lax.rsqrt(total / D + EPS)
            p = teacher()
            for s in range(4):
                v = nt[s, rows, :].astype(F32) * scale
                ns[s, rows, :] = (v * g4[m, s]).astype(BF16)
                nt[s, rows, :] = (v * g4[p, s]).astype(BF16)
            return carry

        lax.fori_loop(0, 8, rows16, 0)

        def turn(s, carry):
            nst[s, :, pl.ds(t * 128, 128)] = ns[s, pl.ds(t * 128, 128), :].T
            return carry

        lax.fori_loop(0, 4, turn, 0)

    def keys(ph, which, s):
        left, out = ((ns, ks), (nt, kt))[which]
        who = m if which == 0 else teacher()
        right = walls[ph][who, s].reshape(SLAB, HALF)
        part = jnp.dot(left[s], right, preferred_element_type=F32)
        if s == 0:
            out[...] = part
        else:
            out[...] += part

    def distill(ph):
        p = teacher()

        def tile(i, carry):
            loss, ggain = carry
            rows = pl.ds(pl.multiple_of(i * 64, 64), 64)
            own_gain, far_gain = g4[m, 4][:, :HD], g4[p, 4][:, :HD]
            for h in range(2):
                cols = pl.ds(h * HD, HD)
                a, b = ks[rows, cols], kt[rows, cols]
                inv_a = lax.rsqrt(jnp.sum(a * a, axis=-1, keepdims=True) / HD + EPS)
                inv_b = lax.rsqrt(jnp.sum(b * b, axis=-1, keepdims=True) / HD + EPS)
                differ = a * inv_a * own_gain - b * inv_b * far_gain
                loss = loss + jnp.sum(differ * differ, axis=0, keepdims=True)
                up = differ / KW
                weighted = up * own_gain
                inner = jnp.sum(weighted * a, axis=-1, keepdims=True)
                g = weighted * inv_a - a * (inv_a * inv_a * inv_a * inner / HD)
                gk[rows, cols] = g.astype(BF16)
                ggain = ggain + jnp.sum(up * a * inv_a, axis=0, keepdims=True)
            return loss, ggain

        zero = jnp.zeros((1, HD), F32)
        loss, ggain = lax.fori_loop(0, TOK // 64, tile, (zero, zero))
        if ph == 0:
            stat4[0, 0:1] = loss
            stat4[0, 1:2] = ggain
        else:
            stat4[0, 0:1] += loss
            stat4[0, 1:2] += ggain

    base1 = [take(6) for _ in range(2)]

    def to_i16(v):
        return ((v + MAGIC) - MAGIC).astype(jnp.int32).astype(I16)

    def top_of(v):
        return jnp.max(jnp.abs(v).reshape(-1, HALF), axis=0, keepdims=True)

    def grads(ph, d):
        s = (x + d) % 4

        def rows320(i, carry):
            rows = pl.ds(pl.multiple_of(i * 320, 320), 320)
            v = jnp.dot(nst[s, rows, :], gk[...], preferred_element_type=F32)
            top = jnp.maximum(top_of(v), 1e-30)
            q[ph, s, i] = to_i16(v * (TOP / top)).reshape(4, CHUNK, HALF)
            sc[ph, s, i] = top / TOP
            return carry

        lax.fori_loop(0, 4, rows320, 0)
        if d < 4:
            send(q.at[ph, s, :, :, ROWS[0]], r1x.at[ph, d - 1], at_x(d), base1[ph])
        for e in (1, 2, 3):
            send(q.at[ph, s, (y + e) % 4, :, ROWS[1]], r1y.at[ph, e - 1, s], at_y(e), base1[ph] + 1)
            send(q.at[ph, s, :, (zl + e) % 4, ROWS[2]], r1z.at[ph, e - 1, s], at_line(e), base1[ph] + 2)

    def grads_send(ph):
        for a, hop in enumerate((at_x, at_y, at_line)):
            for e in (1, 2, 3):
                send(sc.at[ph], s1.at[ph, a, e - 1], hop(e), base1[ph] + 3 + a)

    def wait1(ph, a, ref):
        arrived(ref.at[ph], base1[ph] + a)
        arrived(s1.at[ph, a], base1[ph] + 3 + a)

    def i2f(v):
        return v.astype(jnp.int32).astype(F32)

    def stage2(ph):
        ids = {}
        for a, (own, own_scale, got, got_scale, mid, into, pos, hop, n) in enumerate((
            (lambda i: q[ph, x, i, :, ROWS[0]], lambda i: sc[ph, x, i],
             r1x, lambda d, i: s1[ph, 0, d, x, i], q2x, r2x, y, at_y, 32),
            (lambda i: q[ph, i, y, :, ROWS[1]], lambda i: sc[ph, i, y],
             r1y, lambda d, i: s1[ph, 1, d, i, y], q2y, r2y, x, at_x, 32),
            (lambda i: q[ph, i, :, zl, ROWS[2]], lambda i: sc[ph, i],
             r1z, lambda d, i: s1[ph, 2, d, i], q2z, r2z, x, at_x, 16),
        )):
            wait1(ph, a, got)

            def add(i, top):
                v = i2f(own(i)) * own_scale(i)
                for d in range(3):
                    v = v + i2f(got[ph, d, i]) * got_scale(d, i)
                acc[i, :, 0:n] = v
                return jnp.maximum(top, top_of(v))

            top = lax.fori_loop(0, 4, add, jnp.full((1, HALF), 1e-30, F32))
            factor = TOP / top

            def store(i, carry):
                mid[ph, i] = to_i16(acc[i, :, 0:n] * factor)
                return carry

            lax.fori_loop(0, 4, store, 0)
            s2o[ph, a] = top / TOP
            ids[a] = (take(), take())
            for d in (1, 2, 3):
                send(mid.at[ph, (pos + d) % 4], into.at[ph, d - 1], hop(d), ids[a][0])
                send(s2o.at[ph, a], s2.at[ph, a, d - 1], hop(d), ids[a][1])
        return ids

    def stage3(ph, ids):
        out = {}
        for a, (own, got, mid, into, pos, hop) in enumerate((
            (q2x.at[ph, y], r2x, q3x, r3x, zl, at_line),
            (q2y.at[ph, x], r2y, q3y, r3y, zl, at_line),
            (q2z.at[ph, x], r2z, q3z, r3z, y, at_y),
        )):
            arrived(got.at[ph], ids[a][0])
            arrived(s2.at[ph, a], ids[a][1])
            v = i2f(own[...]) * s2o[ph, a]
            for d in range(3):
                v = v + i2f(got[ph, d]) * s2[ph, a, d]
            top = jnp.maximum(top_of(v), 1e-30)
            mid[ph] = to_i16(v * (TOP / top))
            s3o[ph, a] = top / TOP
            out[a] = (take(), take())
            for d in (1, 2, 3):
                send(mid.at[ph, (pos + d) % 4], into.at[ph, d - 1], hop(d), out[a][0])
                send(s3o.at[ph, a], s3.at[ph, a, d - 1], hop(d), out[a][1])
        return out

    def finish(ph, ids):
        for a, (own, got, n, row) in enumerate((
            (q3x.at[ph, zl], r3x, 32, 0), (q3y.at[ph, zl], r3y, 32, 32), (q3z.at[ph, y], r3z, 16, 64),
        )):
            v = i2f(own[...]) * s3o[ph, a]
            arrived(got.at[ph], ids[a][0])
            arrived(s3.at[ph, a], ids[a][1])
            for d in range(3):
                v = v + i2f(got[ph, d]) * s3[ph, a, d]
            grad[row : row + n, HALF * ph : HALF * ph + HALF] = v

    def stat_send(a, hop):
        ri = take()
        for d in (1, 2, 3):
            send(stat4.at[4 * a], stat4.at[4 * a + d], hop(d), ri)
        return ri

    def stat_add(a, ri):
        arrived(stat4.at[pl.ds(4 * a + 1, 3)], ri)
        return stat4[4 * a] + stat4[4 * a + 1] + stat4[4 * a + 2] + stat4[4 * a + 3]

    for one in loads:
        one.wait()
    first, second = gather(0), gather(1)
    next(first)
    share_gains()
    next(first)
    stat4[0] = jnp.zeros((8, HD), F32)
    pieces = [wait_inputs] + [lambda t=t: prep(t) for t in range(6)]
    step = 0
    for _ in first:
        if pieces:
            pieces.pop(0)()
        step += 1
        if step >= LEAD:
            next(second)

    def work(ph):
        for which in (0, 1):
            for s in range(4):
                yield lambda which=which, s=s: keys(ph, which, s)
        yield lambda: distill(ph)
        for d in (1, 2, 3, 4):
            yield lambda d=d: grads(ph, d)
        yield lambda: grads_send(ph)

    pieces = list(work(0))
    for _ in second:
        if pieces:
            pieces.pop(0)()
    for one in pieces:
        one()
    pieces = list(work(1))
    for one in pieces[:9]:
        one()
    sid = stat_send(0, at_x)
    ids_a = stage2(0)
    for one in pieces[9:11]:
        one()
    stat4[4] = stat_add(0, sid)
    sid = stat_send(1, at_y)
    for one in pieces[11:12]:
        one()
    ids_a = stage3(0, ids_a)
    for one in pieces[12:]:
        one()
    stat4[8] = stat_add(1, sid)
    sid = stat_send(2, at_line)
    finish(0, ids_a)
    ids_b = stage2(1)
    total = stat_add(2, sid)
    loss = jnp.sum(total[0:1], axis=-1, keepdims=True) / float(TOK * 64 * KW)
    ids_b = stage3(1, ids_b)
    stats[...] = jnp.concatenate([jnp.broadcast_to(loss, (1, HD)), total[1:8]], axis=0)
    finish(1, ids_b)
    for one in pending.values():
        one.wait_send()


def local(hidden_in, gain_in, w_key, key_gain, partner):
    vmem, dma = pltpu.VMEM, pltpu.SemaphoreType.DMA
    grad, stats = pl.pallas_call(
        kernel,
        out_shape=(jax.ShapeDtypeStruct((CHUNK, KW), F32), jax.ShapeDtypeStruct((8, HD), F32)),
        in_specs=[
            pl.BlockSpec(memory_space=pl.ANY),
            pl.BlockSpec(memory_space=pltpu.VMEM),
            pl.BlockSpec(memory_space=pltpu.VMEM),
            pl.BlockSpec(memory_space=pl.ANY),
            pl.BlockSpec(memory_space=pltpu.SMEM),
        ],
        out_specs=(pl.BlockSpec(memory_space=pltpu.VMEM), pl.BlockSpec(memory_space=pltpu.VMEM)),
        scratch_shapes=[
            vmem((4, 4, 4, 4, CHUNK, HALF), BF16),
            vmem((4, 4, 4, 4, CHUNK, HALF), BF16),
            vmem((4, TOK, SLAB), BF16),
            vmem((4, TOK, SLAB), BF16),
            vmem((4, SLAB, TOK), BF16),
            vmem((TOK, HALF), F32),
            vmem((TOK, HALF), F32),
            vmem((TOK, HALF), BF16),
            vmem((2, 4, 4, 4, CHUNK, HALF), I16),
            vmem((2, 4, 4, 1, HALF), F32),
            vmem((4, 5, 1, SLAB), F32),
            vmem((12, 8, HD), F32),
            vmem((2, 3, 4, 4, 32, HALF), I16),
            vmem((2, 3, 4, 4, 32, HALF), I16),
            vmem((2, 3, 4, 4, 16, HALF), I16),
            vmem((2, 3, 3, 4, 4, 1, HALF), F32),
            vmem((4, 4, 32, HALF), F32),
            vmem((2, 4, 4, 32, HALF), I16),
            vmem((2, 4, 4, 32, HALF), I16),
            vmem((2, 4, 4, 16, HALF), I16),
            vmem((2, 3, 4, 32, HALF), I16),
            vmem((2, 3, 4, 32, HALF), I16),
            vmem((2, 3, 4, 16, HALF), I16),
            vmem((2, 3, 1, HALF), F32),
            vmem((2, 3, 3, 1, HALF), F32),
            vmem((2, 4, 32, HALF), I16),
            vmem((2, 4, 32, HALF), I16),
            vmem((2, 4, 16, HALF), I16),
            vmem((2, 3, 32, HALF), I16),
            vmem((2, 3, 32, HALF), I16),
            vmem((2, 3, 16, HALF), I16),
            vmem((2, 3, 1, HALF), F32),
            vmem((2, 3, 3, 1, HALF), F32),
            dma((NSEND,)),
            dma((NSEM,)),
            dma((8,)),
        ],
        compiler_params=pltpu.CompilerParams(
            collective_id=0, has_side_effects=True, vmem_limit_bytes=63 * 2**20
        ),
        cost_estimate=pl.CostEstimate(flops=12 * 10**9, bytes_accessed=10**7, transcendentals=0),
    )(hidden_in, gain_in, key_gain, w_key, partner)
    return (grad[None], stats[1:2], stats[0, 0:1])


def solution(mesh):
    return jax.shard_map(
        local,
        mesh=mesh,
        in_specs=(P("mp", "fsdp", None), P("mp", None), P("mp", "fsdp", None), P("mp", None), P()),
        out_specs=(P("mp", "fsdp", None), P("mp", None), P("mp")),
        check_vma=False,
    )
```

```python
import jax
import jax.numpy as jnp
from jax import lax
from jax.experimental import pallas as pl
from jax.experimental.pallas import tpu as pltpu
from jax.sharding import PartitionSpec as P

MESH = pl.DeviceIdType.MESH
F32, BF16, I16 = jnp.float32, jnp.bfloat16, jnp.int16
D, KW, HD, TOK, CHUNK = 5120, 512, 128, 768, 80
HALF = KW // 2
SLAB = D // 4
EPS = 1e-6
TOP = 32767.0
ROWS = (pl.ds(0, 32), pl.ds(32, 32), pl.ds(64, 16))
NSEM = 250
NSEND = 96
LEAD = 10
MAGIC = 12582912.0


def kernel(
    hid, gain, key_gain, w, partner, grad, stats,
    wall0, wall1, ns, nt, nst, ks, kt, gk, q, sc, g4, stat4,
    r1x, r1y, r1z, s1, acc, q2x, q2y, q2z, r2x, r2y, r2z, s2o, s2,
    q3x, q3y, q3z, r3x, r3y, r3z, s3o, s3, ssem, rsem, lsem,
):
    m, f = lax.axis_index("mp"), lax.axis_index("fsdp")
    x, y = f // 16, (f // 4) % 4
    zl, zh, c = f % 4, m // 2, m % 2
    z = zh * 4 + zl

    def dev(px, py, pz, pc):
        pz = (pz + 8) % 8
        return ((pz // 4) * 2 + pc, (((px + 4) % 4) * 4 + (py + 4) % 4) * 4 + pz % 4)

    def at_x(d):
        return dev(x + d, y, z, c)

    def at_y(d):
        return dev(x, y + d, z, c)

    def at_z(d):
        return dev(x, y, z + d, c)

    def at_line(d):
        return dev(x, y, zh * 4 + (zl + d) % 4, c)

    walls = (wall0, wall1)
    sibling = dev(x, y, z, 1 - c)
    others = (sibling, dev(x, y, z + 4, c), dev(x, y, z + 4, 1 - c))
    slot_of = (zh * 2 + 1 - c, (1 - zh) * 2 + c, (1 - zh) * 2 + 1 - c)

    used, sent = [0], [0]
    pending = {}

    def take(n=1):
        used[0] += n
        assert used[0] <= NSEM
        return used[0] - n

    def copy(src, dst, to, si, ri):
        return pltpu.make_async_remote_copy(
            src_ref=src, dst_ref=dst, send_sem=ssem.at[si], recv_sem=rsem.at[ri],
            device_id=to, device_id_type=MESH,
        )

    def send(src, dst, to, ri=None):
        si = sent[0] % NSEND
        sent[0] += 1
        ri = take() if ri is None else ri
        if si in pending:
            pending[si].wait_send()
        one = copy(src, dst, to, si, ri)
        one.start()
        pending[si] = one
        return ri

    def arrived(ref, ri):
        copy(ref, ref, sibling, 0, ri).wait_recv()

    loads = [
        pltpu.make_async_copy(w.at[0, :, pl.ds(HALF * ph, HALF)], walls[ph].at[m, x, y, zl], lsem.at[ph])
        for ph in range(2)
    ]
    for one in loads:
        one.start()
    hidden_loads = [
        pltpu.make_async_copy(hid.at[0, :, pl.ds(SLAB * s, SLAB)], nt.at[s], lsem.at[2 + s]) for s in range(4)
    ]
    for one in hidden_loads:
        one.start()
    barrier = pltpu.get_barrier_semaphore()
    peers = [at_x(d) for d in (1, 2, 3)] + [at_y(d) for d in (1, 2, 3)] + [at_z(1), at_z(-1)]
    peers += [at_line(d) for d in (1, 2, 3)] + list(others)
    for one in peers:
        pl.semaphore_signal(barrier, inc=1, device_id=one, device_id_type=MESH)
    for s in range(4):
        g4[m, s] = gain[:, SLAB * s : SLAB * s + SLAB].astype(F32)
    g4[m, 4] = jnp.zeros((1, SLAB), F32)
    g4[m, 4, :, 0:HD] = key_gain[...].astype(F32)
    pl.semaphore_wait(barrier, len(peers))

    def model(zz):
        return (zz // 4) * 2 + c

    def gather(ph):
        back = take(2)

        def chunk(px, py, part):
            return walls[ph].at[m, px, py, zl, ROWS[part]]

        def block(part, zz, lane=None, half=None):
            some = slice(None) if half is None else pl.ds(2 * half, 2)
            mod, low, rows = model(zz), zz % 4, ROWS[part]
            if lane is None:
                return walls[ph].at[mod, some, :, low, rows]
            lane = (lane + 4) % 4
            if part == 0:
                return walls[ph].at[mod, lane, some, low, rows]
            return walls[ph].at[mod, some, lane, low, rows]

        at = (at_x, at_y)
        pos = (x, y)

        first = {}

        def start(*parts):
            for part in parts:
                mine = chunk(x, y, part)
                hop = at_y if part == 0 else at_x
                first[part] = [send(mine, mine, hop(d)) for d in (1, 2, 3)]

        ring = {}
        last = {}

        def z_own(part, lane):
            mine = block(part, z, lane)
            up = send(mine, mine, at_z(1))
            down = send(mine, mine, at_z(-1))
            ring[part] = (up, down)

        def z_step(part, lane, j):
            up, down = ring[part]
            if j < 4:
                for sign, ri in ((-1, up), (1, down)):
                    got = block(part, (z + sign * j + 8) % 8, lane)
                    arrived(got, ri)
                half = {1: None, 2: None, 3: 0}[j]
                one = block(part, (z - j + 8) % 8, lane, half)
                up = send(one, one, at_z(1))
                half = {1: None, 2: None, 3: 1}[j]
                one = block(part, (z + j) % 8, lane, half)
                down = send(one, one, at_z(-1))
                ring[part] = (up, down)
            else:
                arrived(block(part, (z + 4) % 8, lane, 0), up)
                arrived(block(part, (z + 4) % 8, lane, 1), down)

        def l_own(part, j):
            one = block(part, (z + j + 8) % 8, pos[part])
            last[part, j] = (send(one, one, at[part](1)), send(one, one, at[part](-1)))

        def l_pass(part, j):
            zz = (z + j + 8) % 8
            up, down = last[part, j]
            arrived(block(part, zz, pos[part] - 1), up)
            one = block(part, zz, pos[part] - 1, 0)
            up = send(one, one, at[part](1))
            arrived(block(part, zz, pos[part] + 1), down)
            one = block(part, zz, pos[part] + 1, 1)
            down = send(one, one, at[part](-1))
            last[part, j] = (up, down)

        def hand_over(part, j):
            zz = (z + j + 8) % 8
            one = block(part, zz)
            send(one, one, sibling, back + zz // 4)

        def l_end(part, j):
            zz = (z + j + 8) % 8
            up, down = last[part, j]
            arrived(block(part, zz, pos[part] + 2, 0), up)
            arrived(block(part, zz, pos[part] + 2, 1), down)
            hand_over(part, j)

        second = []

        def z_second():
            for d in (1, 2, 3):
                arrived(chunk((x - d + 4) % 4, y, 2), first[2][d - 1])
            mine = walls[ph].at[m, :, y, zl, ROWS[2]]
            second.extend(send(mine, mine, at_y(d)) for d in (1, 2, 3))

        def z_third():
            for d in (1, 2, 3):
                arrived(walls[ph].at[m, :, (y - d + 4) % 4, zl, ROWS[2]], second[d - 1])
            z_own(2, None)
            hand_over(2, 0)

        def z_ring(j):
            z_step(2, None, j)
            hand_over(2, j)
            if j < 4:
                hand_over(2, -j)

        def own(part):
            for d in (1, 2, 3):
                arrived((chunk(x, (y - d + 4) % 4, 0), chunk((x - d + 4) % 4, y, 1))[part], first[part][d - 1])
            z_own(part, pos[part])
            l_own(part, 0)

        def ring_step(part, j):
            z_step(part, pos[part], j)
            for sign in (-1, 1) if j < 4 else (1,):
                l_own(part, sign * j)

        def line_step(part, j):
            for sign in (-1, 1) if j > 1 else (1,):
                l_pass(part, sign * (j - 1))
            if j > 1:
                for sign in (-1, 1) if j > 2 else (1,):
                    l_end(part, sign * (j - 2))

        def near(part):
            l_pass(part, 4)
            for sign in (-1, 1):
                l_end(part, sign * 3)

        def far(part):
            l_end(part, 4)

        def whole():
            for h in range(2):
                arrived(walls[ph].at[h * 2 + 1 - c], back + h)

        zs = [z_second, z_third] + [lambda j=j: z_ring(j) for j in (1, 2, 3, 4)]
        js = [
            [lambda j=j, part=part: ring_step(part, j) for part in (0, 1)]
            + [lambda j=j, part=part: line_step(part, j) for part in (0, 1)]
            for j in (1, 2, 3, 4)
        ]
        return (
            start, [lambda part=part: own(part) for part in (0, 1)], zs, js,
            [lambda part=part: near(part) for part in (0, 1)], [lambda part=part: far(part) for part in (0, 1)], whole,
        )

    def teacher():
        return partner[m]

    got_gain = []

    def share_gains():
        for to in others:
            got_gain.append(send(g4.at[m], g4.at[m], to))

    def wait_inputs():
        for slot, ri in zip(slot_of, got_gain):
            arrived(g4.at[slot], ri)
        for one in hidden_loads:
            one.wait()

    def prep(t):
        def rows16(i, carry):
            rows = pl.ds(pl.multiple_of(t * 64 + i * 16, 16), 16)
            total = jnp.zeros((16, 1), F32)
            for s in range(4):
                v = nt[s, rows, :].astype(F32)
                total = total + jnp.sum(v * v, axis=-1, keepdims=True)
            scale = lax.rsqrt(total / D + EPS)
            p = teacher()
            for s in range(4):
                v = nt[s, rows, :].astype(F32) * scale
                ns[s, rows, :] = (v * g4[m, s]).astype(BF16)
                nt[s, rows, :] = (v * g4[p, s]).astype(BF16)
            return carry

        lax.fori_loop(0, 4, rows16, 0)

    def transpose(t):
        def turn(s, carry):
            nst[s, :, pl.ds(t * 128, 128)] = ns[s, pl.ds(t * 128, 128), :].T
            return carry

        lax.fori_loop(0, 4, turn, 0)

    def keys(ph, which, s):
        left, out = ((ns, ks), (nt, kt))[which]
        who = m if which == 0 else teacher()
        right = walls[ph][who, s].reshape(SLAB, HALF)
        part = jnp.dot(left[s], right, preferred_element_type=F32)
        if s == 0:
            out[...] = part
        else:
            out[...] += part

    def distill(ph):
        p = teacher()

        def tile(i, carry):
            loss, ggain = carry
            rows = pl.ds(pl.multiple_of(i * 64, 64), 64)
            own_gain, far_gain = g4[m, 4][:, :HD], g4[p, 4][:, :HD]
            for h in range(2):
                cols = pl.ds(h * HD, HD)
                a, b = ks[rows, cols], kt[rows, cols]
                inv_a = lax.rsqrt(jnp.sum(a * a, axis=-1, keepdims=True) / HD + EPS)
                inv_b = lax.rsqrt(jnp.sum(b * b, axis=-1, keepdims=True) / HD + EPS)
                differ = a * inv_a * own_gain - b * inv_b * far_gain
                loss = loss + jnp.sum(differ * differ, axis=0, keepdims=True)
                up = differ / KW
                weighted = up * own_gain
                inner = jnp.sum(weighted * a, axis=-1, keepdims=True)
                g = weighted * inv_a - a * (inv_a * inv_a * inv_a * inner / HD)
                gk[rows, cols] = g.astype(BF16)
                ggain = ggain + jnp.sum(up * a * inv_a, axis=0, keepdims=True)
            return loss, ggain

        zero = jnp.zeros((1, HD), F32)
        loss, ggain = lax.fori_loop(0, TOK // 64, tile, (zero, zero))
        if ph == 0:
            stat4[0, 0:1] = loss
            stat4[0, 1:2] = ggain
        else:
            stat4[0, 0:1] += loss
            stat4[0, 1:2] += ggain

    base1 = [take(6) for _ in range(2)]

    def to_i16(v):
        return ((v + MAGIC) - MAGIC).astype(jnp.int32).astype(I16)

    def top_of(v):
        return jnp.max(jnp.abs(v).reshape(-1, HALF), axis=0, keepdims=True)

    def grads(ph, d):
        s = (x + d) % 4

        def rows320(i, carry):
            rows = pl.ds(pl.multiple_of(i * 320, 320), 320)
            v = jnp.dot(nst[s, rows, :], gk[...], preferred_element_type=F32)
            top = jnp.maximum(top_of(v), 1e-30)
            q[ph, s, i] = to_i16(v * (TOP / top)).reshape(4, CHUNK, HALF)
            sc[ph, s, i] = top / TOP
            return carry

        lax.fori_loop(0, 4, rows320, 0)
        if ph == 0:
            return
        if d < 4:
            send(q.at[ph, s, :, :, ROWS[0]], r1x.at[ph, d - 1], at_x(d), base1[ph])
        for e in (1, 2, 3):
            send(q.at[ph, s, (y + e) % 4, :, ROWS[1]], r1y.at[ph, e - 1, s], at_y(e), base1[ph] + 1)
            send(q.at[ph, s, :, (zl + e) % 4, ROWS[2]], r1z.at[ph, e - 1, s], at_line(e), base1[ph] + 2)

    def send_all(ph):
        for e in (1, 2, 3):
            send(q.at[ph, (x + e) % 4, :, :, ROWS[0]], r1x.at[ph, e - 1], at_x(e), base1[ph])
            send(q.at[ph, :, (y + e) % 4, :, ROWS[1]], r1y.at[ph, e - 1], at_y(e), base1[ph] + 1)
            send(q.at[ph, :, :, (zl + e) % 4, ROWS[2]], r1z.at[ph, e - 1], at_line(e), base1[ph] + 2)
        grads_send(ph)

    def grads_send(ph):
        for a, hop in enumerate((at_x, at_y, at_line)):
            for e in (1, 2, 3):
                send(sc.at[ph], s1.at[ph, a, e - 1], hop(e), base1[ph] + 3 + a)

    def wait1(ph, a, ref):
        arrived(ref.at[ph], base1[ph] + a)
        arrived(s1.at[ph, a], base1[ph] + 3 + a)

    def i2f(v):
        return v.astype(jnp.int32).astype(F32)

    def stage2(ph):
        ids = {}
        for a, (own, own_scale, got, got_scale, mid, into, pos, hop, n) in enumerate((
            (lambda i: q[ph, x, i, :, ROWS[0]], lambda i: sc[ph, x, i],
             r1x, lambda d, i: s1[ph, 0, d, x, i], q2x, r2x, y, at_y, 32),
            (lambda i: q[ph, i, y, :, ROWS[1]], lambda i: sc[ph, i, y],
             r1y, lambda d, i: s1[ph, 1, d, i, y], q2y, r2y, x, at_x, 32),
            (lambda i: q[ph, i, :, zl, ROWS[2]], lambda i: sc[ph, i],
             r1z, lambda d, i: s1[ph, 2, d, i], q2z, r2z, x, at_x, 16),
        )):
            wait1(ph, a, got)

            def add(i, top):
                v = i2f(own(i)) * own_scale(i)
                for d in range(3):
                    v = v + i2f(got[ph, d, i]) * got_scale(d, i)
                acc[i, :, 0:n] = v
                return jnp.maximum(top, top_of(v))

            top = lax.fori_loop(0, 4, add, jnp.full((1, HALF), 1e-30, F32))
            factor = TOP / top

            def store(i, carry):
                mid[ph, i] = to_i16(acc[i, :, 0:n] * factor)
                return carry

            lax.fori_loop(0, 4, store, 0)
            s2o[ph, a] = top / TOP
            ids[a] = (take(), take())
            for d in (1, 2, 3):
                send(mid.at[ph, (pos + d) % 4], into.at[ph, d - 1], hop(d), ids[a][0])
                send(s2o.at[ph, a], s2.at[ph, a, d - 1], hop(d), ids[a][1])
        return ids

    def stage3(ph, ids):
        out = {}
        for a, (own, got, mid, into, pos, hop) in enumerate((
            (q2x.at[ph, y], r2x, q3x, r3x, zl, at_line),
            (q2y.at[ph, x], r2y, q3y, r3y, zl, at_line),
            (q2z.at[ph, x], r2z, q3z, r3z, y, at_y),
        )):
            arrived(got.at[ph], ids[a][0])
            arrived(s2.at[ph, a], ids[a][1])
            v = i2f(own[...]) * s2o[ph, a]
            for d in range(3):
                v = v + i2f(got[ph, d]) * s2[ph, a, d]
            top = jnp.maximum(top_of(v), 1e-30)
            mid[ph] = to_i16(v * (TOP / top))
            s3o[ph, a] = top / TOP
            out[a] = (take(), take())
            for d in (1, 2, 3):
                send(mid.at[ph, (pos + d) % 4], into.at[ph, d - 1], hop(d), out[a][0])
                send(s3o.at[ph, a], s3.at[ph, a, d - 1], hop(d), out[a][1])
        return out

    def finish(ph, ids):
        for a, (own, got, n, row) in enumerate((
            (q3x.at[ph, zl], r3x, 32, 0), (q3y.at[ph, zl], r3y, 32, 32), (q3z.at[ph, y], r3z, 16, 64),
        )):
            v = i2f(own[...]) * s3o[ph, a]
            arrived(got.at[ph], ids[a][0])
            arrived(s3.at[ph, a], ids[a][1])
            for d in range(3):
                v = v + i2f(got[ph, d]) * s3[ph, a, d]
            grad[row : row + n, HALF * ph : HALF * ph + HALF] = v

    def stat_send(a, hop):
        ri = take()
        for d in (1, 2, 3):
            send(stat4.at[4 * a], stat4.at[4 * a + d], hop(d), ri)
        return ri

    def stat_add(a, ri):
        arrived(stat4.at[pl.ds(4 * a + 1, 3)], ri)
        return stat4[4 * a] + stat4[4 * a + 1] + stat4[4 * a + 2] + stat4[4 * a + 3]

    for one in loads:
        one.wait()
    start_a, own_a, z_a, j_a, near_a, far_a, whole_a = gather(0)
    start_b, own_b, z_b, j_b, near_b, far_b, whole_b = gather(1)
    stat4[0] = jnp.zeros((8, HD), F32)
    start_a(2, 0, 1)
    start_b(2)
    share_gains()

    def work(ph):
        return (
            [lambda s=s: keys(ph, 0, s) for s in range(4)],
            [lambda s=s: keys(ph, 1, s) for s in range(4)] + [lambda: distill(ph)],
            [lambda d=d: grads(ph, d) for d in (1, 2, 3, 4)],
        )

    def woven(events, pieces):
        done = 0
        for k, event in enumerate(events):
            event()
            upto = (k + 1) * len(pieces) // len(events)
            for one in pieces[done:upto]:
                one()
            done = upto

    student_a, teacher_a, grads_a = work(0)
    student_b, teacher_b, grads_b = work(1)
    a = [z_a[0]] + own_a + [z_a[1], z_b[0]] + j_a[0] + [z_a[2], z_b[1]] + j_a[1] + [z_a[3], lambda: start_b(0, 1)]
    woven(a, [wait_inputs] + [
        lambda do=do, t=t: do(t) for k in range(6) for do, t in ((prep, 2 * k), (prep, 2 * k + 1), (transpose, k))
    ])
    a = j_a[2] + [z_a[4]] + j_a[3] + near_a + [z_a[5]] + far_a
    b = own_b + [z_b[2]] + j_b[0] + [z_b[3]] + j_b[1]
    early = LEAD
    for one in a[: len(a) - early]:
        one()
    mixed = []
    rest = a[len(a) - early :]
    while rest:
        mixed.append(rest.pop(0))
        if b:
            mixed.append(b.pop(0))
    b = b + [z_b[4]] + j_b[2] + j_b[3] + near_b
    cut = mixed.index(near_a[1]) + 1
    woven(mixed[:cut], [])
    woven(mixed[cut:], student_a)
    b[0]()
    whole_a()
    woven(b[1:], teacher_a + grads_a)
    send_all(0)
    student_b[0]()
    student_b[1]()
    z_b[5]()
    for one in far_b:
        one()
    student_b[2]()
    student_b[3]()
    whole_b()
    for one in teacher_b:
        one()
    sid = stat_send(0, at_x)
    grads_b[0]()
    grads_b[1]()
    ids_a = stage2(0)
    grads_b[2]()
    stat4[4] = stat_add(0, sid)
    sid = stat_send(1, at_y)
    grads_b[3]()
    grads_send(1)
    ids_a = stage3(0, ids_a)
    stat4[8] = stat_add(1, sid)
    sid = stat_send(2, at_line)
    finish(0, ids_a)
    ids_b = stage2(1)
    total = stat_add(2, sid)
    loss = jnp.sum(total[0:1], axis=-1, keepdims=True) / float(TOK * 64 * KW)
    ids_b = stage3(1, ids_b)
    stats[...] = jnp.concatenate([jnp.broadcast_to(loss, (1, HD)), total[1:8]], axis=0)
    finish(1, ids_b)
    for one in pending.values():
        one.wait_send()


def local(hidden_in, gain_in, w_key, key_gain, partner):
    vmem, dma = pltpu.VMEM, pltpu.SemaphoreType.DMA
    grad, stats = pl.pallas_call(
        kernel,
        out_shape=(jax.ShapeDtypeStruct((CHUNK, KW), F32), jax.ShapeDtypeStruct((8, HD), F32)),
        in_specs=[
            pl.BlockSpec(memory_space=pl.ANY),
            pl.BlockSpec(memory_space=pltpu.VMEM),
            pl.BlockSpec(memory_space=pltpu.VMEM),
            pl.BlockSpec(memory_space=pl.ANY),
            pl.BlockSpec(memory_space=pltpu.SMEM),
        ],
        out_specs=(pl.BlockSpec(memory_space=pltpu.VMEM), pl.BlockSpec(memory_space=pltpu.VMEM)),
        scratch_shapes=[
            vmem((4, 4, 4, 4, CHUNK, HALF), BF16),
            vmem((4, 4, 4, 4, CHUNK, HALF), BF16),
            vmem((4, TOK, SLAB), BF16),
            vmem((4, TOK, SLAB), BF16),
            vmem((4, SLAB, TOK), BF16),
            vmem((TOK, HALF), F32),
            vmem((TOK, HALF), F32),
            vmem((TOK, HALF), BF16),
            vmem((2, 4, 4, 4, CHUNK, HALF), I16),
            vmem((2, 4, 4, 1, HALF), F32),
            vmem((4, 5, 1, SLAB), F32),
            vmem((12, 8, HD), F32),
            vmem((2, 3, 4, 4, 32, HALF), I16),
            vmem((2, 3, 4, 4, 32, HALF), I16),
            vmem((2, 3, 4, 4, 16, HALF), I16),
            vmem((2, 3, 3, 4, 4, 1, HALF), F32),
            vmem((4, 4, 32, HALF), F32),
            vmem((2, 4, 4, 32, HALF), I16),
            vmem((2, 4, 4, 32, HALF), I16),
            vmem((2, 4, 4, 16, HALF), I16),
            vmem((2, 3, 4, 32, HALF), I16),
            vmem((2, 3, 4, 32, HALF), I16),
            vmem((2, 3, 4, 16, HALF), I16),
            vmem((2, 3, 1, HALF), F32),
            vmem((2, 3, 3, 1, HALF), F32),
            vmem((2, 4, 32, HALF), I16),
            vmem((2, 4, 32, HALF), I16),
            vmem((2, 4, 16, HALF), I16),
            vmem((2, 3, 32, HALF), I16),
            vmem((2, 3, 32, HALF), I16),
            vmem((2, 3, 16, HALF), I16),
            vmem((2, 3, 1, HALF), F32),
            vmem((2, 3, 3, 1, HALF), F32),
            dma((NSEND,)),
            dma((NSEM,)),
            dma((8,)),
        ],
        compiler_params=pltpu.CompilerParams(
            collective_id=0, has_side_effects=True, vmem_limit_bytes=63 * 2**20
        ),
        cost_estimate=pl.CostEstimate(flops=12 * 10**9, bytes_accessed=10**7, transcendentals=0),
    )(hidden_in, gain_in, key_gain, w_key, partner)
    return (grad[None], stats[1:2], stats[0, 0:1])


def solution(mesh):
    return jax.shard_map(
        local,
        mesh=mesh,
        in_specs=(P("mp", "fsdp", None), P("mp", None), P("mp", "fsdp", None), P("mp", None), P()),
        out_specs=(P("mp", "fsdp", None), P("mp", None), P("mp")),
        check_vma=False,
    )
```

```python
import jax
import jax.numpy as jnp
from jax import lax
from jax.experimental import pallas as pl
from jax.experimental.pallas import tpu as pltpu
from jax.sharding import PartitionSpec as P

MESH = pl.DeviceIdType.MESH
F32, BF16, I16 = jnp.float32, jnp.bfloat16, jnp.int16
D, KW, HD, TOK, CHUNK = 5120, 512, 128, 768, 80
HALF = KW // 2
SLAB = D // 4
EPS = 1e-6
TOP = 32767.0
ROWS = (pl.ds(0, 32), pl.ds(32, 32), pl.ds(64, 16))
NSEM = 254
NSEND = 96
LEAD = 10
MAGIC = 12582912.0


def kernel(
    hid, gain, key_gain, w, partner, grad, stats,
    wall0, wall1, ns, nt, nst, ks, kt, gk, q, sc, g4, gz, stat4,
    r1x, r1y, r1z, s1, acc, q2x, q2y, q2z, r2x, r2y, r2z, s2o, s2,
    q3x, q3y, q3z, r3x, r3y, r3z, s3o, s3, ssem, rsem, lsem,
):
    m, f = lax.axis_index("mp"), lax.axis_index("fsdp")
    x, y = f // 16, (f // 4) % 4
    zl, zh, c = f % 4, m // 2, m % 2
    z = zh * 4 + zl

    def dev(px, py, pz, pc):
        pz = (pz + 8) % 8
        return ((pz // 4) * 2 + pc, (((px + 4) % 4) * 4 + (py + 4) % 4) * 4 + pz % 4)

    def at_x(d):
        return dev(x + d, y, z, c)

    def at_y(d):
        return dev(x, y + d, z, c)

    def at_z(d):
        return dev(x, y, z + d, c)

    def at_line(d):
        return dev(x, y, zh * 4 + (zl + d) % 4, c)

    walls = (wall0, wall1)
    sibling = dev(x, y, z, 1 - c)
    far_half = (1 - zh) * 2 + c

    used, sent = [0], [0]
    pending = {}

    def take(n=1):
        used[0] += n
        assert used[0] <= NSEM
        return used[0] - n

    def copy(src, dst, to, si, ri):
        return pltpu.make_async_remote_copy(
            src_ref=src, dst_ref=dst, send_sem=ssem.at[si], recv_sem=rsem.at[ri],
            device_id=to, device_id_type=MESH,
        )

    def send(src, dst, to, ri=None):
        si = sent[0] % NSEND
        sent[0] += 1
        ri = take() if ri is None else ri
        if si in pending:
            pending[si].wait_send()
        one = copy(src, dst, to, si, ri)
        one.start()
        pending[si] = one
        return ri

    def arrived(ref, ri):
        copy(ref, ref, sibling, 0, ri).wait_recv()

    loads = [
        pltpu.make_async_copy(w.at[0, :, pl.ds(HALF * ph, HALF)], walls[ph].at[m, x, y, zl], lsem.at[ph])
        for ph in range(2)
    ]
    for one in loads:
        one.start()
    hidden_loads = [
        pltpu.make_async_copy(hid.at[0, :, pl.ds(SLAB * s, SLAB)], nt.at[s], lsem.at[2 + s]) for s in range(4)
    ]
    for one in hidden_loads:
        one.start()
    barrier = pltpu.get_barrier_semaphore()
    peers = [at_x(d) for d in (1, 2, 3)] + [at_y(d) for d in (1, 2, 3)] + [at_z(1), at_z(-1)]
    peers += [at_line(d) for d in (1, 2, 3)] + [sibling]
    for one in peers:
        pl.semaphore_signal(barrier, inc=1, device_id=one, device_id_type=MESH)
    for s in range(4):
        g4[m, s] = gain[:, SLAB * s : SLAB * s + SLAB].astype(F32)
    g4[m, 4] = jnp.zeros((1, SLAB), F32)
    g4[m, 4, :, 0:HD] = key_gain[...].astype(F32)
    pl.semaphore_wait(barrier, len(peers))

    def model(zz):
        return (zz // 4) * 2 + c

    def gather(ph):
        back = take(2)

        def chunk(px, py, part):
            return walls[ph].at[m, px, py, zl, ROWS[part]]

        def block(part, zz, lane=None, half=None):
            some = slice(None) if half is None else pl.ds(2 * half, 2)
            mod, low, rows = model(zz), zz % 4, ROWS[part]
            if lane is None:
                return walls[ph].at[mod, some, :, low, rows]
            lane = (lane + 4) % 4
            if part == 0:
                return walls[ph].at[mod, lane, some, low, rows]
            return walls[ph].at[mod, some, lane, low, rows]

        at = (at_x, at_y)
        pos = (x, y)

        first = {}

        def start(*parts):
            for part in parts:
                mine = chunk(x, y, part)
                hop = at_y if part == 0 else at_x
                first[part] = [send(mine, mine, hop(d)) for d in (1, 2, 3)]

        ring = {}
        last = {}

        def z_own(part, lane):
            mine = block(part, z, lane)
            up = send(mine, mine, at_z(1))
            down = send(mine, mine, at_z(-1))
            ring[part] = (up, down)

        def z_step(part, lane, j):
            up, down = ring[part]
            if j < 4:
                for sign, ri in ((-1, up), (1, down)):
                    got = block(part, (z + sign * j + 8) % 8, lane)
                    arrived(got, ri)
                half = {1: None, 2: None, 3: 0}[j]
                one = block(part, (z - j + 8) % 8, lane, half)
                up = send(one, one, at_z(1))
                half = {1: None, 2: None, 3: 1}[j]
                one = block(part, (z + j) % 8, lane, half)
                down = send(one, one, at_z(-1))
                ring[part] = (up, down)
            else:
                arrived(block(part, (z + 4) % 8, lane, 0), up)
                arrived(block(part, (z + 4) % 8, lane, 1), down)

        def l_own(part, j):
            one = block(part, (z + j + 8) % 8, pos[part])
            last[part, j] = (send(one, one, at[part](1)), send(one, one, at[part](-1)))

        def l_pass(part, j):
            zz = (z + j + 8) % 8
            up, down = last[part, j]
            arrived(block(part, zz, pos[part] - 1), up)
            one = block(part, zz, pos[part] - 1, 0)
            up = send(one, one, at[part](1))
            arrived(block(part, zz, pos[part] + 1), down)
            one = block(part, zz, pos[part] + 1, 1)
            down = send(one, one, at[part](-1))
            last[part, j] = (up, down)

        def hand_over(part, j):
            zz = (z + j + 8) % 8
            one = block(part, zz)
            send(one, one, sibling, back + zz // 4)

        def l_end(part, j):
            zz = (z + j + 8) % 8
            up, down = last[part, j]
            arrived(block(part, zz, pos[part] + 2, 0), up)
            arrived(block(part, zz, pos[part] + 2, 1), down)
            hand_over(part, j)

        second = []

        def z_second():
            for d in (1, 2, 3):
                arrived(chunk((x - d + 4) % 4, y, 2), first[2][d - 1])
            mine = walls[ph].at[m, :, y, zl, ROWS[2]]
            second.extend(send(mine, mine, at_y(d)) for d in (1, 2, 3))

        def z_third():
            for d in (1, 2, 3):
                arrived(walls[ph].at[m, :, (y - d + 4) % 4, zl, ROWS[2]], second[d - 1])
            z_own(2, None)
            hand_over(2, 0)

        def z_ring(j):
            z_step(2, None, j)
            hand_over(2, j)
            if j < 4:
                hand_over(2, -j)

        def own(part):
            for d in (1, 2, 3):
                arrived((chunk(x, (y - d + 4) % 4, 0), chunk((x - d + 4) % 4, y, 1))[part], first[part][d - 1])
            z_own(part, pos[part])
            l_own(part, 0)

        def ring_step(part, j):
            z_step(part, pos[part], j)
            for sign in (-1, 1) if j < 4 else (1,):
                l_own(part, sign * j)

        def line_step(part, j):
            for sign in (-1, 1) if j > 1 else (1,):
                l_pass(part, sign * (j - 1))
            if j > 1:
                for sign in (-1, 1) if j > 2 else (1,):
                    l_end(part, sign * (j - 2))

        def near(part):
            l_pass(part, 4)
            for sign in (-1, 1):
                l_end(part, sign * 3)

        def far(part):
            l_end(part, 4)

        def whole():
            for h in range(2):
                arrived(walls[ph].at[h * 2 + 1 - c], back + h)

        zs = [z_second, z_third] + [lambda j=j: z_ring(j) for j in (1, 2, 3, 4)]
        js = [
            [lambda j=j, part=part: ring_step(part, j) for part in (0, 1)]
            + [lambda j=j, part=part: line_step(part, j) for part in (0, 1)]
            for j in (1, 2, 3, 4)
        ]
        return (
            start, [lambda part=part: own(part) for part in (0, 1)], zs, js,
            [lambda part=part: near(part) for part in (0, 1)], [lambda part=part: far(part) for part in (0, 1)], whole,
        )

    def teacher():
        return partner[m]

    got_gain = []

    def share_gains():
        got_gain.append(send(g4.at[m], gz.at[0], at_z(1)))
        got_gain.append(send(g4.at[m], gz.at[1], at_z(-1)))

    def pass_gains():
        arrived(gz.at[0], got_gain[0])
        got_gain.append(send(gz.at[0], gz.at[2], at_z(1)))
        arrived(gz.at[1], got_gain[1])
        got_gain.append(send(gz.at[1], gz.at[4], at_z(-1)))

    def hand_gains():
        arrived(gz.at[2], got_gain[2])
        arrived(gz.at[4], got_gain[3])
        g4[far_half] = gz[(zl * 2) % 5]
        got_gain.append(send(g4.at[m], g4.at[m], sibling))
        got_gain.append(send(g4.at[far_half], g4.at[far_half], sibling))

    def wait_inputs():
        arrived(g4.at[zh * 2 + 1 - c], got_gain[4])
        arrived(g4.at[(1 - zh) * 2 + 1 - c], got_gain[5])
        for one in hidden_loads:
            one.wait()

    def prep(t):
        def rows16(i, carry):
            rows = pl.ds(pl.multiple_of(t * 64 + i * 16, 16), 16)
            total = jnp.zeros((16, 1), F32)
            for s in range(4):
                v = nt[s, rows, :].astype(F32)
                total = total + jnp.sum(v * v, axis=-1, keepdims=True)
            scale = lax.rsqrt(total / D + EPS)
            p = teacher()
            for s in range(4):
                v = nt[s, rows, :].astype(F32) * scale
                ns[s, rows, :] = (v * g4[m, s]).astype(BF16)
                nt[s, rows, :] = (v * g4[p, s]).astype(BF16)
            return carry

        lax.fori_loop(0, 4, rows16, 0)

    def transpose(t):
        def turn(s, carry):
            nst[s, :, pl.ds(t * 128, 128)] = ns[s, pl.ds(t * 128, 128), :].T
            return carry

        lax.fori_loop(0, 4, turn, 0)

    def keys(ph, which, s):
        left, out = ((ns, ks), (nt, kt))[which]
        who = m if which == 0 else teacher()
        right = walls[ph][who, s].reshape(SLAB, HALF)
        part = jnp.dot(left[s], right, preferred_element_type=F32)
        if s == 0:
            out[...] = part
        else:
            out[...] += part

    def distill(ph):
        p = teacher()

        def tile(i, carry):
            loss, ggain = carry
            rows = pl.ds(pl.multiple_of(i * 64, 64), 64)
            own_gain, far_gain = g4[m, 4][:, :HD], g4[p, 4][:, :HD]
            for h in range(2):
                cols = pl.ds(h * HD, HD)
                a, b = ks[rows, cols], kt[rows, cols]
                inv_a = lax.rsqrt(jnp.sum(a * a, axis=-1, keepdims=True) / HD + EPS)
                inv_b = lax.rsqrt(jnp.sum(b * b, axis=-1, keepdims=True) / HD + EPS)
                differ = a * inv_a * own_gain - b * inv_b * far_gain
                loss = loss + jnp.sum(differ * differ, axis=0, keepdims=True)
                up = differ / KW
                weighted = up * own_gain
                inner = jnp.sum(weighted * a, axis=-1, keepdims=True)
                g = weighted * inv_a - a * (inv_a * inv_a * inv_a * inner / HD)
                gk[rows, cols] = g.astype(BF16)
                ggain = ggain + jnp.sum(up * a * inv_a, axis=0, keepdims=True)
            return loss, ggain

        zero = jnp.zeros((1, HD), F32)
        loss, ggain = lax.fori_loop(0, TOK // 64, tile, (zero, zero))
        if ph == 0:
            stat4[0, 0:1] = loss
            stat4[0, 1:2] = ggain
        else:
            stat4[0, 0:1] += loss
            stat4[0, 1:2] += ggain

    base1 = [take(6) for _ in range(2)]

    def to_i16(v):
        return ((v + MAGIC) - MAGIC).astype(jnp.int32).astype(I16)

    def top_of(v):
        return jnp.max(jnp.abs(v).reshape(-1, HALF), axis=0, keepdims=True)

    def grads(ph, d):
        s = (x + d) % 4

        def rows320(i, carry):
            rows = pl.ds(pl.multiple_of(i * 320, 320), 320)
            v = jnp.dot(nst[s, rows, :], gk[...], preferred_element_type=F32)
            top = jnp.maximum(top_of(v), 1e-30)
            q[ph, s, i] = to_i16(v * (TOP / top)).reshape(4, CHUNK, HALF)
            sc[ph, s, i] = top / TOP
            return carry

        lax.fori_loop(0, 4, rows320, 0)
        if ph == 0:
            return
        if d < 4:
            send(q.at[ph, s, :, :, ROWS[0]], r1x.at[ph, d - 1], at_x(d), base1[ph])
        for e in (1, 2, 3):
            send(q.at[ph, s, (y + e) % 4, :, ROWS[1]], r1y.at[ph, e - 1, s], at_y(e), base1[ph] + 1)
            send(q.at[ph, s, :, (zl + e) % 4, ROWS[2]], r1z.at[ph, e - 1, s], at_line(e), base1[ph] + 2)

    def send_all(ph):
        for e in (1, 2, 3):
            send(q.at[ph, (x + e) % 4, :, :, ROWS[0]], r1x.at[ph, e - 1], at_x(e), base1[ph])
            send(q.at[ph, :, (y + e) % 4, :, ROWS[1]], r1y.at[ph, e - 1], at_y(e), base1[ph] + 1)
            send(q.at[ph, :, :, (zl + e) % 4, ROWS[2]], r1z.at[ph, e - 1], at_line(e), base1[ph] + 2)
        grads_send(ph)

    def grads_send(ph):
        for a, hop in enumerate((at_x, at_y, at_line)):
            for e in (1, 2, 3):
                send(sc.at[ph], s1.at[ph, a, e - 1], hop(e), base1[ph] + 3 + a)

    def wait1(ph, a, ref):
        arrived(ref.at[ph], base1[ph] + a)
        arrived(s1.at[ph, a], base1[ph] + 3 + a)

    def i2f(v):
        return v.astype(jnp.int32).astype(F32)

    def stage2(ph):
        ids = {}
        for a, (own, own_scale, got, got_scale, mid, into, pos, hop, n) in enumerate((
            (lambda i: q[ph, x, i, :, ROWS[0]], lambda i: sc[ph, x, i],
             r1x, lambda d, i: s1[ph, 0, d, x, i], q2x, r2x, y, at_y, 32),
            (lambda i: q[ph, i, y, :, ROWS[1]], lambda i: sc[ph, i, y],
             r1y, lambda d, i: s1[ph, 1, d, i, y], q2y, r2y, x, at_x, 32),
            (lambda i: q[ph, i, :, zl, ROWS[2]], lambda i: sc[ph, i],
             r1z, lambda d, i: s1[ph, 2, d, i], q2z, r2z, x, at_x, 16),
        )):
            wait1(ph, a, got)

            def add(i, top):
                v = i2f(own(i)) * own_scale(i)
                for d in range(3):
                    v = v + i2f(got[ph, d, i]) * got_scale(d, i)
                acc[i, :, 0:n] = v
                return jnp.maximum(top, top_of(v))

            top = lax.fori_loop(0, 4, add, jnp.full((1, HALF), 1e-30, F32))
            factor = TOP / top

            def store(i, carry):
                mid[ph, i] = to_i16(acc[i, :, 0:n] * factor)
                return carry

            lax.fori_loop(0, 4, store, 0)
            s2o[ph, a] = top / TOP
            ids[a] = (take(), take())
            for d in (1, 2, 3):
                send(mid.at[ph, (pos + d) % 4], into.at[ph, d - 1], hop(d), ids[a][0])
                send(s2o.at[ph, a], s2.at[ph, a, d - 1], hop(d), ids[a][1])
        return ids

    def stage3(ph, ids):
        out = {}
        for a, (own, got, mid, into, pos, hop) in enumerate((
            (q2x.at[ph, y], r2x, q3x, r3x, zl, at_line),
            (q2y.at[ph, x], r2y, q3y, r3y, zl, at_line),
            (q2z.at[ph, x], r2z, q3z, r3z, y, at_y),
        )):
            arrived(got.at[ph], ids[a][0])
            arrived(s2.at[ph, a], ids[a][1])
            v = i2f(own[...]) * s2o[ph, a]
            for d in range(3):
                v = v + i2f(got[ph, d]) * s2[ph, a, d]
            top = jnp.maximum(top_of(v), 1e-30)
            mid[ph] = to_i16(v * (TOP / top))
            s3o[ph, a] = top / TOP
            out[a] = (take(), take())
            for d in (1, 2, 3):
                send(mid.at[ph, (pos + d) % 4], into.at[ph, d - 1], hop(d), out[a][0])
                send(s3o.at[ph, a], s3.at[ph, a, d - 1], hop(d), out[a][1])
        return out

    def finish(ph, ids):
        for a, (own, got, n, row) in enumerate((
            (q3x.at[ph, zl], r3x, 32, 0), (q3y.at[ph, zl], r3y, 32, 32), (q3z.at[ph, y], r3z, 16, 64),
        )):
            v = i2f(own[...]) * s3o[ph, a]
            arrived(got.at[ph], ids[a][0])
            arrived(s3.at[ph, a], ids[a][1])
            for d in range(3):
                v = v + i2f(got[ph, d]) * s3[ph, a, d]
            grad[row : row + n, HALF * ph : HALF * ph + HALF] = v

    def stat_send(a, hop):
        ri = take()
        for d in (1, 2, 3):
            send(stat4.at[4 * a], stat4.at[4 * a + d], hop(d), ri)
        return ri

    def stat_add(a, ri):
        arrived(stat4.at[pl.ds(4 * a + 1, 3)], ri)
        return stat4[4 * a] + stat4[4 * a + 1] + stat4[4 * a + 2] + stat4[4 * a + 3]

    for one in loads:
        one.wait()
    start_a, own_a, z_a, j_a, near_a, far_a, whole_a = gather(0)
    start_b, own_b, z_b, j_b, near_b, far_b, whole_b = gather(1)
    stat4[0] = jnp.zeros((8, HD), F32)
    start_a(2, 0, 1)
    start_b(2)
    share_gains()

    def work(ph):
        return (
            [lambda s=s: keys(ph, 0, s) for s in range(4)],
            [lambda s=s: keys(ph, 1, s) for s in range(4)] + [lambda: distill(ph)],
            [lambda d=d: grads(ph, d) for d in (1, 2, 3, 4)],
        )

    def woven(events, pieces):
        done = 0
        for k, event in enumerate(events):
            event()
            upto = (k + 1) * len(pieces) // len(events)
            for one in pieces[done:upto]:
                one()
            done = upto

    student_a, teacher_a, grads_a = work(0)
    student_b, teacher_b, grads_b = work(1)
    a = [z_a[0]] + own_a + [z_a[1], z_b[0]] + j_a[0] + [z_a[2], z_b[1]] + j_a[1] + [z_a[3], lambda: start_b(0, 1)]
    opening = a
    a = j_a[2] + [z_a[4]] + j_a[3] + near_a + [z_a[5]] + far_a
    b = own_b + [z_b[2]] + j_b[0] + [z_b[3]] + j_b[1]
    early = LEAD
    opening = opening + a[: len(a) - early]
    mixed = []
    rest = a[len(a) - early :]
    while rest:
        mixed.append(rest.pop(0))
        if b:
            mixed.append(b.pop(0))
    b = b + [z_b[4]] + j_b[2] + j_b[3] + near_b
    cut = mixed.index(near_a[1]) + 1
    woven(opening + mixed[:cut], [pass_gains, hand_gains, wait_inputs] + [
        lambda do=do, t=t: do(t) for k in range(6) for do, t in ((prep, 2 * k), (prep, 2 * k + 1), (transpose, k))
    ])
    woven(mixed[cut:], student_a)
    b[0]()
    whole_a()
    woven(b[1:], teacher_a + grads_a)
    send_all(0)
    student_b[0]()
    student_b[1]()
    z_b[5]()
    for one in far_b:
        one()
    student_b[2]()
    student_b[3]()
    whole_b()
    for one in teacher_b:
        one()
    sid = stat_send(0, at_x)
    grads_b[0]()
    grads_b[1]()
    ids_a = stage2(0)
    grads_b[2]()
    stat4[4] = stat_add(0, sid)
    sid = stat_send(1, at_y)
    grads_b[3]()
    grads_send(1)
    ids_a = stage3(0, ids_a)
    stat4[8] = stat_add(1, sid)
    sid = stat_send(2, at_line)
    finish(0, ids_a)
    ids_b = stage2(1)
    total = stat_add(2, sid)
    loss = jnp.sum(total[0:1], axis=-1, keepdims=True) / float(TOK * 64 * KW)
    ids_b = stage3(1, ids_b)
    stats[...] = jnp.concatenate([jnp.broadcast_to(loss, (1, HD)), total[1:8]], axis=0)
    finish(1, ids_b)
    for one in pending.values():
        one.wait_send()


def local(hidden_in, gain_in, w_key, key_gain, partner):
    vmem, dma = pltpu.VMEM, pltpu.SemaphoreType.DMA
    grad, stats = pl.pallas_call(
        kernel,
        out_shape=(jax.ShapeDtypeStruct((CHUNK, KW), F32), jax.ShapeDtypeStruct((8, HD), F32)),
        in_specs=[
            pl.BlockSpec(memory_space=pl.ANY),
            pl.BlockSpec(memory_space=pltpu.VMEM),
            pl.BlockSpec(memory_space=pltpu.VMEM),
            pl.BlockSpec(memory_space=pl.ANY),
            pl.BlockSpec(memory_space=pltpu.SMEM),
        ],
        out_specs=(pl.BlockSpec(memory_space=pltpu.VMEM), pl.BlockSpec(memory_space=pltpu.VMEM)),
        scratch_shapes=[
            vmem((4, 4, 4, 4, CHUNK, HALF), BF16),
            vmem((4, 4, 4, 4, CHUNK, HALF), BF16),
            vmem((4, TOK, SLAB), BF16),
            vmem((4, TOK, SLAB), BF16),
            vmem((4, SLAB, TOK), BF16),
            vmem((TOK, HALF), F32),
            vmem((TOK, HALF), F32),
            vmem((TOK, HALF), BF16),
            vmem((2, 4, 4, 4, CHUNK, HALF), I16),
            vmem((2, 4, 4, 1, HALF), F32),
            vmem((4, 5, 1, SLAB), F32),
            vmem((5, 5, 1, SLAB), F32),
            vmem((12, 8, HD), F32),
            vmem((2, 3, 4, 4, 32, HALF), I16),
            vmem((2, 3, 4, 4, 32, HALF), I16),
            vmem((2, 3, 4, 4, 16, HALF), I16),
            vmem((2, 3, 3, 4, 4, 1, HALF), F32),
            vmem((4, 4, 32, HALF), F32),
            vmem((2, 4, 4, 32, HALF), I16),
            vmem((2, 4, 4, 32, HALF), I16),
            vmem((2, 4, 4, 16, HALF), I16),
            vmem((2, 3, 4, 32, HALF), I16),
            vmem((2, 3, 4, 32, HALF), I16),
            vmem((2, 3, 4, 16, HALF), I16),
            vmem((2, 3, 1, HALF), F32),
            vmem((2, 3, 3, 1, HALF), F32),
            vmem((2, 4, 32, HALF), I16),
            vmem((2, 4, 32, HALF), I16),
            vmem((2, 4, 16, HALF), I16),
            vmem((2, 3, 32, HALF), I16),
            vmem((2, 3, 32, HALF), I16),
            vmem((2, 3, 16, HALF), I16),
            vmem((2, 3, 1, HALF), F32),
            vmem((2, 3, 3, 1, HALF), F32),
            dma((NSEND,)),
            dma((NSEM,)),
            dma((8,)),
        ],
        compiler_params=pltpu.CompilerParams(
            collective_id=0, has_side_effects=True, vmem_limit_bytes=63 * 2**20
        ),
        cost_estimate=pl.CostEstimate(flops=12 * 10**9, bytes_accessed=10**7, transcendentals=0),
    )(hidden_in, gain_in, key_gain, w_key, partner)
    return (grad[None], stats[1:2], stats[0, 0:1])


def solution(mesh):
    return jax.shard_map(
        local,
        mesh=mesh,
        in_specs=(P("mp", "fsdp", None), P("mp", None), P("mp", "fsdp", None), P("mp", None), P()),
        out_specs=(P("mp", "fsdp", None), P("mp", None), P("mp")),
        check_vma=False,
    )
```

```python
import jax
import jax.numpy as jnp
from jax import lax
from jax.experimental import pallas as pl
from jax.experimental.pallas import tpu as pltpu
from jax.sharding import PartitionSpec as P

MESH = pl.DeviceIdType.MESH
F32, BF16, I16 = jnp.float32, jnp.bfloat16, jnp.int16
D, KW, HD, TOK, CHUNK = 5120, 512, 128, 768, 80
HALF = KW // 2
SLAB = D // 4
EPS = 1e-6
TOP = 32767.0
ROWS = (pl.ds(0, 32), pl.ds(32, 32), pl.ds(64, 16))
NSEM = 254
NSEND = 96
LEAD = 10
MAGIC = 12582912.0


def kernel(
    hid, gain, key_gain, w, partner, grad, stats,
    wall0, wall1, ns, nt, nst, ks, kt, gk, q, sc, g4, gz, stat4,
    r1x, r1y, r1z, s1, acc, q2x, q2y, q2z, r2x, r2y, r2z, s2o, s2,
    q3x, q3y, q3z, r3x, r3y, r3z, s3o, s3, ssem, rsem, lsem,
):
    m, f = lax.axis_index("mp"), lax.axis_index("fsdp")
    x, y = f // 16, (f // 4) % 4
    zl, zh, c = f % 4, m // 2, m % 2
    z = zh * 4 + zl

    def dev(px, py, pz, pc):
        pz = (pz + 8) % 8
        return ((pz // 4) * 2 + pc, (((px + 4) % 4) * 4 + (py + 4) % 4) * 4 + pz % 4)

    def at_x(d):
        return dev(x + d, y, z, c)

    def at_y(d):
        return dev(x, y + d, z, c)

    def at_z(d):
        return dev(x, y, z + d, c)

    def at_line(d):
        return dev(x, y, zh * 4 + (zl + d) % 4, c)

    walls = (wall0, wall1)
    sibling = dev(x, y, z, 1 - c)
    far_half = (1 - zh) * 2 + c

    used, sent = [0], [0]
    pending = {}

    def take(n=1):
        used[0] += n
        assert used[0] <= NSEM
        return used[0] - n

    def copy(src, dst, to, si, ri):
        return pltpu.make_async_remote_copy(
            src_ref=src, dst_ref=dst, send_sem=ssem.at[si], recv_sem=rsem.at[ri],
            device_id=to, device_id_type=MESH,
        )

    def send(src, dst, to, ri=None):
        si = sent[0] % NSEND
        sent[0] += 1
        ri = take() if ri is None else ri
        if si in pending:
            pending[si].wait_send()
        one = copy(src, dst, to, si, ri)
        one.start()
        pending[si] = one
        return ri

    def arrived(ref, ri):
        copy(ref, ref, sibling, 0, ri).wait_recv()

    loads = [
        pltpu.make_async_copy(w.at[0, :, pl.ds(HALF * ph, HALF)], walls[ph].at[m, x, y, zl], lsem.at[ph])
        for ph in range(2)
    ]
    for one in loads:
        one.start()
    hidden_loads = [
        pltpu.make_async_copy(hid.at[0, :, pl.ds(SLAB * s, SLAB)], nt.at[s], lsem.at[2 + s]) for s in range(4)
    ]
    for one in hidden_loads:
        one.start()
    barrier = pltpu.get_barrier_semaphore()
    peers = [at_x(d) for d in (1, 2, 3)] + [at_y(d) for d in (1, 2, 3)] + [at_z(1), at_z(-1)]
    peers += [at_line(d) for d in (1, 2, 3)] + [sibling]
    for one in peers:
        pl.semaphore_signal(barrier, inc=1, device_id=one, device_id_type=MESH)
    for s in range(4):
        g4[m, s] = gain[:, SLAB * s : SLAB * s + SLAB].astype(F32)
    g4[m, 4] = jnp.zeros((1, SLAB), F32)
    g4[m, 4, :, 0:HD] = key_gain[...].astype(F32)
    pl.semaphore_wait(barrier, len(peers))

    def model(zz):
        return (zz // 4) * 2 + c

    def gather(ph):
        back = take(2)

        def chunk(px, py, part):
            return walls[ph].at[m, px, py, zl, ROWS[part]]

        def block(part, zz, lane=None, half=None):
            some = slice(None) if half is None else pl.ds(2 * half, 2)
            mod, low, rows = model(zz), zz % 4, ROWS[part]
            if lane is None:
                return walls[ph].at[mod, some, :, low, rows]
            lane = (lane + 4) % 4
            if part == 0:
                return walls[ph].at[mod, lane, some, low, rows]
            return walls[ph].at[mod, some, lane, low, rows]

        at = (at_x, at_y)
        pos = (x, y)

        first = {}

        def start(*parts):
            for part in parts:
                mine = chunk(x, y, part)
                hop = at_y if part == 0 else at_x
                first[part] = [send(mine, mine, hop(d)) for d in (1, 2, 3)]

        ring = {}
        last = {}

        def z_own(part, lane):
            mine = block(part, z, lane)
            up = send(mine, mine, at_z(1))
            down = send(mine, mine, at_z(-1))
            ring[part] = (up, down)

        def z_step(part, lane, j):
            up, down = ring[part]
            if j < 4:
                for sign, ri in ((-1, up), (1, down)):
                    got = block(part, (z + sign * j + 8) % 8, lane)
                    arrived(got, ri)
                half = {1: None, 2: None, 3: 0}[j]
                one = block(part, (z - j + 8) % 8, lane, half)
                up = send(one, one, at_z(1))
                half = {1: None, 2: None, 3: 1}[j]
                one = block(part, (z + j) % 8, lane, half)
                down = send(one, one, at_z(-1))
                ring[part] = (up, down)
            else:
                arrived(block(part, (z + 4) % 8, lane, 0), up)
                arrived(block(part, (z + 4) % 8, lane, 1), down)

        def l_own(part, j):
            one = block(part, (z + j + 8) % 8, pos[part])
            last[part, j] = (send(one, one, at[part](1)), send(one, one, at[part](-1)))

        def l_pass(part, j):
            zz = (z + j + 8) % 8
            up, down = last[part, j]
            arrived(block(part, zz, pos[part] - 1), up)
            one = block(part, zz, pos[part] - 1, 0)
            up = send(one, one, at[part](1))
            arrived(block(part, zz, pos[part] + 1), down)
            one = block(part, zz, pos[part] + 1, 1)
            down = send(one, one, at[part](-1))
            last[part, j] = (up, down)

        def hand_over(part, j):
            zz = (z + j + 8) % 8
            one = block(part, zz)
            send(one, one, sibling, back + zz // 4)

        def l_end(part, j):
            zz = (z + j + 8) % 8
            up, down = last[part, j]
            arrived(block(part, zz, pos[part] + 2, 0), up)
            arrived(block(part, zz, pos[part] + 2, 1), down)
            hand_over(part, j)

        second = []

        def z_second():
            for d in (1, 2, 3):
                arrived(chunk((x - d + 4) % 4, y, 2), first[2][d - 1])
            mine = walls[ph].at[m, :, y, zl, ROWS[2]]
            second.extend(send(mine, mine, at_y(d)) for d in (1, 2, 3))

        def z_third():
            for d in (1, 2, 3):
                arrived(walls[ph].at[m, :, (y - d + 4) % 4, zl, ROWS[2]], second[d - 1])
            z_own(2, None)
            hand_over(2, 0)

        def z_ring(j):
            z_step(2, None, j)
            hand_over(2, j)
            if j < 4:
                hand_over(2, -j)

        def own(part):
            for d in (1, 2, 3):
                arrived((chunk(x, (y - d + 4) % 4, 0), chunk((x - d + 4) % 4, y, 1))[part], first[part][d - 1])
            z_own(part, pos[part])
            l_own(part, 0)

        def ring_step(part, j):
            z_step(part, pos[part], j)
            for sign in (-1, 1) if j < 4 else (1,):
                l_own(part, sign * j)

        def line_step(part, j):
            for sign in (-1, 1) if j > 1 else (1,):
                l_pass(part, sign * (j - 1))
            if j > 1:
                for sign in (-1, 1) if j > 2 else (1,):
                    l_end(part, sign * (j - 2))

        def near(part):
            l_pass(part, 4)
            for sign in (-1, 1):
                l_end(part, sign * 3)

        def far(part):
            l_end(part, 4)

        def whole():
            for h in range(2):
                arrived(walls[ph].at[h * 2 + 1 - c], back + h)

        zs = [z_second, z_third] + [lambda j=j: z_ring(j) for j in (1, 2, 3, 4)]
        js = [
            [lambda j=j, part=part: ring_step(part, j) for part in (0, 1)]
            + [lambda j=j, part=part: line_step(part, j) for part in (0, 1)]
            for j in (1, 2, 3, 4)
        ]
        return (
            start, [lambda part=part: own(part) for part in (0, 1)], zs, js,
            [lambda part=part: near(part) for part in (0, 1)], [lambda part=part: far(part) for part in (0, 1)], whole,
        )

    def teacher():
        return partner[m]

    got_gain = []

    def share_gains():
        got_gain.append(send(g4.at[m], gz.at[0], at_z(1)))
        got_gain.append(send(g4.at[m], gz.at[1], at_z(-1)))

    def pass_gains():
        arrived(gz.at[0], got_gain[0])
        got_gain.append(send(gz.at[0], gz.at[2], at_z(1)))
        arrived(gz.at[1], got_gain[1])
        got_gain.append(send(gz.at[1], gz.at[4], at_z(-1)))

    def hand_gains():
        arrived(gz.at[2], got_gain[2])
        arrived(gz.at[4], got_gain[3])
        g4[far_half] = gz[(zl * 2) % 5]
        got_gain.append(send(g4.at[m], g4.at[m], sibling))
        got_gain.append(send(g4.at[far_half], g4.at[far_half], sibling))

    def wait_inputs():
        arrived(g4.at[zh * 2 + 1 - c], got_gain[4])
        arrived(g4.at[(1 - zh) * 2 + 1 - c], got_gain[5])
        for one in hidden_loads:
            one.wait()

    def prep(t):
        def rows16(i, carry):
            rows = pl.ds(pl.multiple_of(t * 64 + i * 16, 16), 16)
            total = jnp.zeros((16, 1), F32)
            for s in range(4):
                v = nt[s, rows, :].astype(F32)
                total = total + jnp.sum(v * v, axis=-1, keepdims=True)
            scale = lax.rsqrt(total / D + EPS)
            p = teacher()
            for s in range(4):
                v = nt[s, rows, :].astype(F32) * scale
                ns[s, rows, :] = (v * g4[m, s]).astype(BF16)
                nt[s, rows, :] = (v * g4[p, s]).astype(BF16)
            return carry

        lax.fori_loop(0, 4, rows16, 0)

    def transpose(t):
        def turn(s, carry):
            nst[s, :, pl.ds(t * 128, 128)] = ns[s, pl.ds(t * 128, 128), :].T
            return carry

        lax.fori_loop(0, 4, turn, 0)

    def keys(ph, which, s):
        left, out = ((ns, ks), (nt, kt))[which]
        who = m if which == 0 else teacher()
        right = walls[ph][who, s].reshape(SLAB, HALF)
        part = jnp.dot(left[s], right, preferred_element_type=F32)
        if s == 0:
            out[...] = part
        else:
            out[...] += part

    def distill(ph):
        p = teacher()

        def tile(i, carry):
            loss, ggain = carry
            rows = pl.ds(pl.multiple_of(i * 64, 64), 64)
            own_gain, far_gain = g4[m, 4][:, :HD], g4[p, 4][:, :HD]
            for h in range(2):
                cols = pl.ds(h * HD, HD)
                a, b = ks[rows, cols], kt[rows, cols]
                inv_a = lax.rsqrt(jnp.sum(a * a, axis=-1, keepdims=True) / HD + EPS)
                inv_b = lax.rsqrt(jnp.sum(b * b, axis=-1, keepdims=True) / HD + EPS)
                differ = a * inv_a * own_gain - b * inv_b * far_gain
                loss = loss + jnp.sum(differ * differ, axis=0, keepdims=True)
                up = differ / KW
                weighted = up * own_gain
                inner = jnp.sum(weighted * a, axis=-1, keepdims=True)
                g = weighted * inv_a - a * (inv_a * inv_a * inv_a * inner / HD)
                gk[rows, cols] = g.astype(BF16)
                ggain = ggain + jnp.sum(up * a * inv_a, axis=0, keepdims=True)
            return loss, ggain

        zero = jnp.zeros((1, HD), F32)
        loss, ggain = lax.fori_loop(0, TOK // 64, tile, (zero, zero))
        if ph == 0:
            stat4[0, 0:1] = loss
            stat4[0, 1:2] = ggain
        else:
            stat4[0, 0:1] += loss
            stat4[0, 1:2] += ggain

    base1 = [take(6) for _ in range(2)]

    def to_i16(v):
        return ((v + MAGIC) - MAGIC).astype(jnp.int32).astype(I16)

    def top_of(v):
        return jnp.max(jnp.abs(v).reshape(-1, HALF), axis=0, keepdims=True)

    def grads(ph, d):
        s = (x + d) % 4

        def rows320(i, carry):
            rows = pl.ds(pl.multiple_of(i * 320, 320), 320)
            v = jnp.dot(nst[s, rows, :], gk[...], preferred_element_type=F32)
            top = jnp.maximum(top_of(v), 1e-30)
            q[ph, s, i] = to_i16(v * (TOP / top)).reshape(4, CHUNK, HALF)
            sc[ph, s, i] = top / TOP
            return carry

        lax.fori_loop(0, 4, rows320, 0)
        if ph == 0:
            return
        if d < 4:
            send(q.at[ph, s, :, :, ROWS[0]], r1x.at[ph, d - 1], at_x(d), base1[ph])
        for e in (1, 2, 3):
            send(q.at[ph, s, (y + e) % 4, :, ROWS[1]], r1y.at[ph, e - 1, s], at_y(e), base1[ph] + 1)
            send(q.at[ph, s, :, (zl + e) % 4, ROWS[2]], r1z.at[ph, e - 1, s], at_line(e), base1[ph] + 2)

    def send_all(ph):
        for e in (1, 2, 3):
            send(q.at[ph, (x + e) % 4, :, :, ROWS[0]], r1x.at[ph, e - 1], at_x(e), base1[ph])
            send(q.at[ph, :, (y + e) % 4, :, ROWS[1]], r1y.at[ph, e - 1], at_y(e), base1[ph] + 1)
            send(q.at[ph, :, :, (zl + e) % 4, ROWS[2]], r1z.at[ph, e - 1], at_line(e), base1[ph] + 2)
        grads_send(ph)

    def grads_send(ph):
        for a, hop in enumerate((at_x, at_y, at_line)):
            for e in (1, 2, 3):
                send(sc.at[ph], s1.at[ph, a, e - 1], hop(e), base1[ph] + 3 + a)

    def wait1(ph, a, ref):
        arrived(ref.at[ph], base1[ph] + a)
        arrived(s1.at[ph, a], base1[ph] + 3 + a)

    def i2f(v):
        return v.astype(jnp.int32).astype(F32)

    def stage2(ph):
        ids = {}
        for a, (own, own_scale, got, got_scale, mid, into, pos, hop, n) in enumerate((
            (lambda i: q[ph, x, i, :, ROWS[0]], lambda i: sc[ph, x, i],
             r1x, lambda d, i: s1[ph, 0, d, x, i], q2x, r2x, y, at_y, 32),
            (lambda i: q[ph, i, y, :, ROWS[1]], lambda i: sc[ph, i, y],
             r1y, lambda d, i: s1[ph, 1, d, i, y], q2y, r2y, x, at_x, 32),
            (lambda i: q[ph, i, :, zl, ROWS[2]], lambda i: sc[ph, i],
             r1z, lambda d, i: s1[ph, 2, d, i], q2z, r2z, x, at_x, 16),
        )):
            wait1(ph, a, got)

            def add(i, top):
                v = i2f(own(i)) * own_scale(i)
                for d in range(3):
                    v = v + i2f(got[ph, d, i]) * got_scale(d, i)
                acc[i, :, 0:n] = v
                return jnp.maximum(top, top_of(v))

            top = lax.fori_loop(0, 4, add, jnp.full((1, HALF), 1e-30, F32))
            factor = TOP / top

            def store(i, carry):
                mid[ph, i] = to_i16(acc[i, :, 0:n] * factor)
                return carry

            lax.fori_loop(0, 4, store, 0)
            s2o[ph, a] = top / TOP
            ids[a] = (take(), take())
            for d in (1, 2, 3):
                send(mid.at[ph, (pos + d) % 4], into.at[ph, d - 1], hop(d), ids[a][0])
                send(s2o.at[ph, a], s2.at[ph, a, d - 1], hop(d), ids[a][1])
        return ids

    def stage3(ph, ids):
        out = {}
        for a, (own, got, mid, into, pos, hop) in enumerate((
            (q2x.at[ph, y], r2x, q3x, r3x, zl, at_line),
            (q2y.at[ph, x], r2y, q3y, r3y, zl, at_line),
            (q2z.at[ph, x], r2z, q3z, r3z, y, at_y),
        )):
            arrived(got.at[ph], ids[a][0])
            arrived(s2.at[ph, a], ids[a][1])
            v = i2f(own[...]) * s2o[ph, a]
            for d in range(3):
                v = v + i2f(got[ph, d]) * s2[ph, a, d]
            top = jnp.maximum(top_of(v), 1e-30)
            mid[ph] = to_i16(v * (TOP / top))
            s3o[ph, a] = top / TOP
            out[a] = (take(), take())
            for d in (1, 2, 3):
                send(mid.at[ph, (pos + d) % 4], into.at[ph, d - 1], hop(d), out[a][0])
                send(s3o.at[ph, a], s3.at[ph, a, d - 1], hop(d), out[a][1])
        return out

    def finish(ph, ids):
        for a, (own, got, n, row) in enumerate((
            (q3x.at[ph, zl], r3x, 32, 0), (q3y.at[ph, zl], r3y, 32, 32), (q3z.at[ph, y], r3z, 16, 64),
        )):
            v = i2f(own[...]) * s3o[ph, a]
            arrived(got.at[ph], ids[a][0])
            arrived(s3.at[ph, a], ids[a][1])
            for d in range(3):
                v = v + i2f(got[ph, d]) * s3[ph, a, d]
            grad[row : row + n, HALF * ph : HALF * ph + HALF] = v

    def stat_send(a, hop):
        ri = take()
        for d in (1, 2, 3):
            send(stat4.at[4 * a], stat4.at[4 * a + d], hop(d), ri)
        return ri

    def stat_add(a, ri):
        arrived(stat4.at[pl.ds(4 * a + 1, 3)], ri)
        return stat4[4 * a] + stat4[4 * a + 1] + stat4[4 * a + 2] + stat4[4 * a + 3]

    for one in loads:
        one.wait()
    start_a, own_a, z_a, j_a, near_a, far_a, whole_a = gather(0)
    start_b, own_b, z_b, j_b, near_b, far_b, whole_b = gather(1)
    stat4[0] = jnp.zeros((8, HD), F32)
    start_a(2, 0, 1)
    start_b(2)
    share_gains()

    def work(ph):
        return (
            [lambda s=s: keys(ph, 0, s) for s in range(4)],
            [lambda s=s: keys(ph, 1, s) for s in range(4)] + [lambda: distill(ph)],
            [lambda d=d: grads(ph, d) for d in (1, 2, 3, 4)],
        )

    def woven(events, pieces):
        done = 0
        for k, event in enumerate(events):
            event()
            upto = (k + 1) * len(pieces) // len(events)
            for one in pieces[done:upto]:
                one()
            done = upto

    student_a, teacher_a, grads_a = work(0)
    student_b, teacher_b, grads_b = work(1)
    a = [z_a[0]] + own_a + [z_a[1], z_b[0]] + j_a[0] + [z_a[2], z_b[1]] + j_a[1] + [z_a[3], lambda: start_b(0, 1)]
    opening = a
    a = j_a[2] + [z_a[4]] + j_a[3] + near_a + [z_a[5]] + far_a
    b = own_b + [z_b[2]] + j_b[0] + [z_b[3]] + j_b[1]
    early = LEAD
    opening = opening + a[: len(a) - early]
    mixed = []
    rest = a[len(a) - early :]
    while rest:
        mixed.append(rest.pop(0))
        if b:
            mixed.append(b.pop(0))
    b = b + [z_b[4]] + j_b[2] + j_b[3] + near_b
    cut = mixed.index(near_a[1]) + 1
    woven(opening + mixed[:cut], [pass_gains, hand_gains, wait_inputs] + [
        lambda do=do, t=t: do(t) for k in range(6) for do, t in ((prep, 2 * k), (prep, 2 * k + 1), (transpose, k))
    ])
    woven(mixed[cut:], student_a)
    b[0]()
    whole_a()
    woven(b[1:], teacher_a + grads_a)
    send_all(0)
    student_b[0]()
    student_b[1]()
    z_b[5]()
    for one in far_b:
        one()
    student_b[2]()
    student_b[3]()
    whole_b()
    for one in teacher_b:
        one()
    sid = stat_send(0, at_x)
    grads_b[0]()
    ids_a = stage2(0)
    grads_b[1]()
    grads_b[2]()
    stat4[4] = stat_add(0, sid)
    sid = stat_send(1, at_y)
    grads_b[3]()
    grads_send(1)
    ids_a = stage3(0, ids_a)
    stat4[8] = stat_add(1, sid)
    sid = stat_send(2, at_line)
    finish(0, ids_a)
    ids_b = stage2(1)
    total = stat_add(2, sid)
    loss = jnp.sum(total[0:1], axis=-1, keepdims=True) / float(TOK * 64 * KW)
    ids_b = stage3(1, ids_b)
    stats[...] = jnp.concatenate([jnp.broadcast_to(loss, (1, HD)), total[1:8]], axis=0)
    finish(1, ids_b)
    for one in pending.values():
        one.wait_send()


def local(hidden_in, gain_in, w_key, key_gain, partner):
    vmem, dma = pltpu.VMEM, pltpu.SemaphoreType.DMA
    grad, stats = pl.pallas_call(
        kernel,
        out_shape=(jax.ShapeDtypeStruct((CHUNK, KW), F32), jax.ShapeDtypeStruct((8, HD), F32)),
        in_specs=[
            pl.BlockSpec(memory_space=pl.ANY),
            pl.BlockSpec(memory_space=pltpu.VMEM),
            pl.BlockSpec(memory_space=pltpu.VMEM),
            pl.BlockSpec(memory_space=pl.ANY),
            pl.BlockSpec(memory_space=pltpu.SMEM),
        ],
        out_specs=(pl.BlockSpec(memory_space=pltpu.VMEM), pl.BlockSpec(memory_space=pltpu.VMEM)),
        scratch_shapes=[
            vmem((4, 4, 4, 4, CHUNK, HALF), BF16),
            vmem((4, 4, 4, 4, CHUNK, HALF), BF16),
            vmem((4, TOK, SLAB), BF16),
            vmem((4, TOK, SLAB), BF16),
            vmem((4, SLAB, TOK), BF16),
            vmem((TOK, HALF), F32),
            vmem((TOK, HALF), F32),
            vmem((TOK, HALF), BF16),
            vmem((2, 4, 4, 4, CHUNK, HALF), I16),
            vmem((2, 4, 4, 1, HALF), F32),
            vmem((4, 5, 1, SLAB), F32),
            vmem((5, 5, 1, SLAB), F32),
            vmem((12, 8, HD), F32),
            vmem((2, 3, 4, 4, 32, HALF), I16),
            vmem((2, 3, 4, 4, 32, HALF), I16),
            vmem((2, 3, 4, 4, 16, HALF), I16),
            vmem((2, 3, 3, 4, 4, 1, HALF), F32),
            vmem((4, 4, 32, HALF), F32),
            vmem((2, 4, 4, 32, HALF), I16),
            vmem((2, 4, 4, 32, HALF), I16),
            vmem((2, 4, 4, 16, HALF), I16),
            vmem((2, 3, 4, 32, HALF), I16),
            vmem((2, 3, 4, 32, HALF), I16),
            vmem((2, 3, 4, 16, HALF), I16),
            vmem((2, 3, 1, HALF), F32),
            vmem((2, 3, 3, 1, HALF), F32),
            vmem((2, 4, 32, HALF), I16),
            vmem((2, 4, 32, HALF), I16),
            vmem((2, 4, 16, HALF), I16),
            vmem((2, 3, 32, HALF), I16),
            vmem((2, 3, 32, HALF), I16),
            vmem((2, 3, 16, HALF), I16),
            vmem((2, 3, 1, HALF), F32),
            vmem((2, 3, 3, 1, HALF), F32),
            dma((NSEND,)),
            dma((NSEM,)),
            dma((8,)),
        ],
        compiler_params=pltpu.CompilerParams(
            collective_id=0, has_side_effects=True, vmem_limit_bytes=63 * 2**20
        ),
        cost_estimate=pl.CostEstimate(flops=12 * 10**9, bytes_accessed=10**7, transcendentals=0),
    )(hidden_in, gain_in, key_gain, w_key, partner)
    return (grad[None], stats[1:2], stats[0, 0:1])


def solution(mesh):
    return jax.shard_map(
        local,
        mesh=mesh,
        in_specs=(P("mp", "fsdp", None), P("mp", None), P("mp", "fsdp", None), P("mp", None), P()),
        out_specs=(P("mp", "fsdp", None), P("mp", None), P("mp")),
        check_vma=False,
    )
```
